128 devices in a mesh: face: 4 (over y), tile: 32 (over z, x, core).
Axes of the slice: x: 4, y: 4, z: 4, core: 2. Of those that a mesh axis runs over, the one named last changes fastest.
Arguments:
- state: bfloat16 [4, 32, 8, 256, 512], P('face', 'tile'), as said below
- obs_feat: bfloat16 [393216, 128], P(('face', 'tile')), may hold values from -6 to 6
- obs_dest: int32 [393216, 1], P(('face', 'tile')), may hold values from 0 to 127; in each aligned block of 3072 rows (0 to 3071, 3072 to 6143, ...) at most 96 rows name the same one
- obs_cell: int32 [393216], P(('face', 'tile')), may hold values from 0 to 2047
- obs_weight: bfloat16 [128, 512], replicated, may hold values from -0.5 to 0.5
- obs_bias: float32 [512], replicated, may hold values from -3 to 3
- obs_gain: float32 [512], replicated, may hold values from 0.5 to 2
- norm_gain: float32 [512], replicated, may hold values from 0.1 to 1.9
- conv_weight: bfloat16 [9, 512, 512], replicated, may hold values from -0.25 to 0.25
- mlp_gain: float32 [512], replicated, may hold values from 0.1 to 1.9
- mlp_in: bfloat16 [512, 2048], replicated, may hold values from -0.25 to 0.25
- mlp_out: bfloat16 [2048, 512], replicated, may hold values from -0.125 to 0.125
Outputs:
- encoded: bfloat16 [4, 32, 8, 256, 512], P('face', 'tile')
The draws below stay inside these ranges and needn't reach their ends.
Inputs may be any that keep to these rules, and one draw needn't show every extreme that they name: `obs_dest`: among the rows of one device no strip is named by more than 96 rows, a bound that some block reaches of them. `state`: cell scales differ from cell to cell and channel to channel.
All inputs are finite; a program needn't handle non-finite values.
Results may differ from the reference program's by a relative error of at most 0.0085.
Values may be sent and summed in bfloat16 or wider, within the bound.
A program may use at most 128 MiB of HBM per device.

```python
import math
import jax
import jax.numpy as jnp
import numpy as np
from jax import lax

C = 512
F = 128
FFN = 2048
BR = 8
OBS_DEV = 3072
S = 256
CAP = 96
OBS = 393216
N_FACE = 4
N_TILE = 32
DEVICES = 128


def draw_state(key, part):
    key = jax.random.fold_in(key, 7)
    key_base, key_cell, key_chan = jax.random.split(key, 3)
    shape = (N_FACE, N_TILE, BR, S, C)
    cell_scale = jnp.exp(jax.random.uniform(key_cell, (N_FACE, N_TILE, BR, S, 1), jnp.float32, 0.0, math.log(10.0)))
    chan_scale = jnp.exp(jax.random.uniform(key_chan, (C,), jnp.float32, 0.0, math.log(3.0)))
    base = jax.random.normal(key_base, shape, jnp.float32)
    return (base * cell_scale * chan_scale * 0.05).astype(jnp.bfloat16)


def touch_ends(values, own_key, least, high):
    place = [jax.random.randint(jax.random.fold_in(own_key, axis), (), 0, length) for axis, length in enumerate(values.shape)]
    main_axis = values.shape.index(max(values.shape))
    next_to = place[:main_axis] + [(place[main_axis] + 1) % values.shape[main_axis]] + place[main_axis + 1:]
    return values.at[tuple(place)].set(least).at[tuple(next_to)].set(high)


def steps_of(rng, dims, shards, smallest, largest):
    factor_of, own = 1.0, jax.random.fold_in(rng, 6)
    for dim, parts in shards:
        heights = jnp.exp(jax.random.uniform(jax.random.fold_in(own, dim), (parts,), jnp.float32, smallest / len(shards), largest / len(shards)))
        factor_of = factor_of * jnp.repeat(heights, dims[dim] // parts).reshape([-1 if axis == dim else 1 for axis in range(len(dims))])
    return factor_of


def shared_out(stream_key, own, number, rows, count, top, most, slope):
    ranking = jax.random.permutation(stream_key, count)
    heavy_load, common = portions_of(count, rows * top, most, slope, True), portions_of(count, rows * top, most, slope, False)
    places = jnp.arange(count)

    def named(sizes, offset_by):
        used = int((sizes > 0).sum())
        fixed = max(1, used // 4)
        passed = fixed + (places - fixed + offset_by * (used - fixed)) % max(1, count - fixed)
        return jnp.zeros((count,), jnp.int32).at[ranking[jnp.where(places < fixed, places, passed)]].set(jnp.asarray(sizes, jnp.int32))

    sizes = jnp.where(number % 4 == 0, named(heavy_load, number // 4), named(common, number - number // 4 - 1))
    mixed = jax.random.permutation(jax.random.fold_in(own, 3), count)
    source_of, receiver = mixed[0:count // 2 * 2:2], mixed[1:count // 2 * 2:2]
    slack = jnp.minimum(sizes[source_of] - 1, most - sizes[receiver]) // 2
    slack = jnp.where((source_of == ranking[0]) | (receiver == ranking[0]) | (sizes[receiver] == 0), 0, jnp.maximum(slack, 0))
    passed = jax.random.randint(jax.random.fold_in(own, 4), (count // 2,), 0, 1 << 20) % (slack + 1)
    sizes = sizes.at[source_of].add(-passed).at[receiver].add(passed)
    labels = jnp.searchsorted(jnp.cumsum(sizes), jnp.arange(rows * top), side="right").astype(jnp.int32)
    listing = labels.reshape(top, rows).T
    listing = listing[jax.random.permutation(jax.random.fold_in(own, 1), rows)]
    offset_by = jax.random.randint(jax.random.fold_in(own, 2), (rows, 1), 0, top)
    return jnp.take_along_axis(listing, (jnp.arange(top)[None, :] + offset_by) % top, axis=1)


def portions_of(amount, total, reach, lean, full):
    loads = [(1 << 20) // math.isqrt(standing ** lean) + 1 for standing in range(1, amount + 1)]
    largest = reach if full else min(reach, max(-(-total // amount), total * loads[0] // sum(loads)))
    least = 1 if total - largest >= amount - 1 else 0
    given, spare = [largest] + [least] * (amount - 1), total - largest - least * (amount - 1)
    while spare > 0:
        movable = [i for i in range(1, amount) if given[i] < largest] or [i for i in range(1, amount) if given[i] < reach]
        whole, remaining = sum([loads[i] for i in movable]), spare
        for i in movable:
            more = min(reach - given[i], max(1, remaining * loads[i] // whole), spare)
            given[i] = given[i] + more
            spare = spare - more
    return np.array(given)


def noise(stream_key, shape, deviation, bound, cuts=(), kind=jnp.bfloat16):
    loudness = steps_of(stream_key, shape, cuts, -0.22, 0.18) if cuts else 1.0
    values = jax.random.normal(stream_key, shape, jnp.float32) * deviation * loudness
    return jnp.minimum(jnp.maximum(values, -bound), bound).astype(kind)


def setup_inputs(seed: int = 0) -> dict:
    arg_keys = jax.random.split(jax.random.key(seed), 13)
    state = draw_state(jax.random.fold_in(arg_keys[12], 71), 0)
    obs_feat = noise(arg_keys[1], (OBS, F), 1.0, 6.0, ((0, 128),))
    obs_dest_keys = jax.random.split(jax.random.fold_in(arg_keys[2], 1), OBS // OBS_DEV)
    obs_dest_turns = jax.random.permutation(jax.random.fold_in(arg_keys[2], 3), OBS // OBS_DEV)
    obs_dest = jax.vmap(lambda own, number: shared_out(jax.random.fold_in(arg_keys[2], 2), own, number, OBS_DEV, DEVICES, 1, CAP, 2))(obs_dest_keys, obs_dest_turns).reshape((OBS, 1))
    obs_cell = touch_ends(jax.random.randint(arg_keys[3], (OBS,), 0, BR * S), jax.random.fold_in(arg_keys[3], 1), 0, (BR * S) - 1).astype(jnp.int32)
    obs_weight = noise(arg_keys[4], (F, C), F ** -0.5, 0.5)
    obs_bias = noise(arg_keys[5], (C,), 0.5, 3.0, (), jnp.float32)
    obs_gain = jnp.clip(jnp.exp(jax.random.uniform(arg_keys[6], (C,), jnp.float32, math.log(0.5), math.log(2.0))), 0.5, 2.0)
    norm_gain = jnp.clip(1.0 + 0.18 * jax.random.normal(arg_keys[7], (C,), jnp.float32), 0.1, 1.9)
    conv_weight = noise(arg_keys[8], (9, C, C), C ** -0.5, 0.25)
    mlp_gain = jnp.clip(1.0 + 0.18 * jax.random.normal(arg_keys[9], (C,), jnp.float32), 0.1, 1.9)
    mlp_in = noise(arg_keys[10], (C, FFN), C ** -0.5, 0.25)
    mlp_out = noise(arg_keys[11], (FFN, C), FFN ** -0.5, 0.125)
    return {"state": state, "obs_feat": obs_feat, "obs_dest": obs_dest, "obs_cell": obs_cell, "obs_weight": obs_weight, "obs_bias": obs_bias, "obs_gain": obs_gain, "norm_gain": norm_gain, "conv_weight": conv_weight, "mlp_gain": mlp_gain, "mlp_in": mlp_in, "mlp_out": mlp_out}


def rms_norm(values, gain):
    scale = lax.rsqrt(lax.optimization_barrier(jnp.mean(values * values, axis=-1, keepdims=True)) + 1e-05)
    return values * scale * gain.astype(jnp.float32)

def reference(state, obs_feat, obs_dest, obs_cell, obs_weight, obs_bias, obs_gain, norm_gain, conv_weight, mlp_gain, mlp_in, mlp_out):
    dev_count = N_FACE * N_TILE
    cell_count = BR * S
    width = state.shape[-1]
    target = obs_dest[:, 0] * cell_count + obs_cell
    feat_blocks = obs_feat.reshape(dev_count, OBS_DEV, obs_feat.shape[1])
    target_blocks = target.reshape(dev_count, OBS_DEV)

    def accumulate(carry, item):
        feats, spots = item
        embed = jax.nn.gelu(jnp.dot(feats, obs_weight, preferred_element_type=jnp.float32) + obs_bias).astype(jnp.bfloat16)
        sums = carry[0].at[spots].add(embed.astype(jnp.float32))
        counts = carry[1].at[spots].add(jnp.ones(spots.shape, jnp.float32))
        return ((sums, counts), None)
    init = (jnp.zeros((dev_count * cell_count, width), jnp.float32), jnp.zeros((dev_count * cell_count,), jnp.float32))
    (total, count), _ = lax.scan(accumulate, init, (feat_blocks, target_blocks))
    mean_obs = total / jnp.maximum(count, 1.0)[:, None]
    grid = (state.astype(jnp.float32) + obs_gain * mean_obs.reshape(state.shape)).astype(jnp.bfloat16)
    normed = rms_norm(grid.astype(jnp.float32), norm_gain).astype(jnp.bfloat16)
    side = N_TILE * BR
    face = normed.reshape(4, side, side, width)
    padded = jnp.pad(face, ((0, 0), (1, 1), (1, 1), (0, 0)))
    following = jnp.roll(face, -1, axis=0)
    preceding = jnp.roll(face, 1, axis=0)
    padded = padded.at[:, 1:side + 1, side + 1].set(following[:, 0, ::-1, :])
    padded = padded.at[:, 0, 1:side + 1].set(preceding[:, ::-1, side - 1, :])
    conv = jnp.zeros((4 * side * side, width), jnp.float32)
    for tap_row in range(3):
        for tap_col in range(3):
            window = padded[:, tap_row:tap_row + side, tap_col:tap_col + side].reshape(-1, width)
            conv = conv + jnp.dot(window, conv_weight[3 * tap_row + tap_col], preferred_element_type=jnp.float32)
    conv = conv.reshape(state.shape)
    mid = grid.astype(jnp.float32) + conv
    normed_two = rms_norm(mid, mlp_gain).astype(jnp.bfloat16)
    hidden = jax.nn.gelu(jnp.dot(normed_two.reshape(-1, width), mlp_in, preferred_element_type=jnp.float32)).astype(jnp.bfloat16)
    result = mid + jnp.dot(hidden, mlp_out, preferred_element_type=jnp.float32).reshape(mid.shape)
    return result.astype(jnp.bfloat16)
```

```python
import math

import jax
import jax.numpy as jnp
from jax import lax
from jax.experimental import pallas as pl
from jax.experimental.pallas import tpu as pltpu
from jax.sharding import PartitionSpec as P

BF16 = jnp.bfloat16
F32 = jnp.float32
I32 = jnp.int32
MESH = pl.DeviceIdType.MESH
EPS = 1e-05
MIB = 2**20
UNIT = 16
BLOCK = 256


def gelu(x):
    inner = x * (math.sqrt(2.0 / math.pi) + (0.044715 * math.sqrt(2.0 / math.pi)) * (x * x))
    half = 0.5 * x
    return half + half * jnp.tanh(inner)


def ones_where(mask):
    return jnp.where(mask, 1.0, 0.0)


def dot(a, b):
    return jnp.dot(a, b, preferred_element_type=F32)


def dot_lanes(a, b):
    return lax.dot_general(a, b, (((1,), (1,)), ((), ())), preferred_element_type=F32)


def rank_kernel(dest, cell, rank, starts, cells):
    devices = starts.shape[1]
    rows = dest.shape[1]
    hot = lax.broadcasted_iota(I32, (devices, rows), 0) == dest[...]
    hot_f = ones_where(hot)
    hot_b = hot_f.astype(BF16)
    before = ones_where(
        lax.broadcasted_iota(I32, (BLOCK, BLOCK), 0) < lax.broadcasted_iota(I32, (BLOCK, BLOCK), 1)
    ).astype(BF16)
    ahead = jnp.zeros((devices, 1), F32)
    pieces = []
    for block in range(rows // BLOCK):
        at = slice(block * BLOCK, (block + 1) * BLOCK)
        pieces.append(dot(hot_b[:, at], before) + ahead)
        ahead = ahead + jnp.sum(hot_f[:, at], axis=1, keepdims=True)
    earlier = jnp.concatenate(pieces, axis=1)
    row_id = lax.broadcasted_iota(I32, (devices, devices), 0)
    col_id = lax.broadcasted_iota(I32, (devices, devices), 1)
    start = dot(
        ones_where(col_id < row_id).astype(BF16),
        jnp.broadcast_to(ahead, (devices, devices)).astype(BF16),
    )
    starts[...] = jnp.sum(jnp.where(row_id == col_id, start, 0.0), axis=0, keepdims=True).astype(I32)
    rank_in = jnp.sum(hot_f * earlier, axis=0, keepdims=True).astype(I32)
    rank[...] = jnp.sum(hot_f * (earlier + start[:, :1]), axis=0, keepdims=True).astype(I32)
    spot = cell[...] + 1
    high = hot_f * (spot // 128).astype(F32)
    low = hot_f * (spot % 128).astype(F32)
    in_slot = ones_where(lax.broadcasted_iota(I32, (128, rows), 0) == rank_in).astype(BF16)
    split = dot_lanes(jnp.concatenate([high, low], axis=0).astype(BF16), in_slot)
    cells[...] = (split[:devices] * 128.0 + split[devices:]).astype(I32)


def cut_kernel(starts, rank, feat, send, ordered):
    devices = send.shape[0]
    rows = feat.shape[0]
    capacity = send.shape[1] * send.shape[2]

    def sort_block(block, _):
        first = pl.multiple_of(block * BLOCK, BLOCK)
        chosen = ones_where(
            lax.broadcasted_iota(I32, (BLOCK, rows), 0) + first == rank[...]
        ).astype(BF16)
        ordered[pl.ds(first, BLOCK), :] = dot(chosen, feat[...])
        return 0

    lax.fori_loop(0, rows // BLOCK, sort_block, 0)
    ordered[rows:, :] = jnp.zeros((ordered.shape[0] - rows, feat.shape[1]), F32)

    def cut(target, _):
        values = ordered[pl.ds(starts[0, target], capacity), :]
        send[target] = values.astype(BF16).reshape(send.shape[1:])
        return 0

    lax.fori_loop(0, devices, cut, 0, unroll=4)


def pack(dest, cell, feat, devices, capacity):
    rows, width = feat.shape
    vmem = pl.BlockSpec(memory_space=pltpu.VMEM)
    rank, starts, cells = pl.pallas_call(
        rank_kernel,
        out_shape=(
            jax.ShapeDtypeStruct((1, rows), I32),
            jax.ShapeDtypeStruct((1, devices), I32),
            jax.ShapeDtypeStruct((devices, 128), I32),
        ),
        in_specs=[vmem] * 2,
        out_specs=[vmem] * 3,
        compiler_params=pltpu.CompilerParams(vmem_limit_bytes=40 * MIB),
        name="rank",
    )(dest, cell)
    send = pl.pallas_call(
        cut_kernel,
        out_shape=jax.ShapeDtypeStruct((devices, capacity // UNIT, UNIT, width), BF16),
        in_specs=[pl.BlockSpec(memory_space=pltpu.SMEM), vmem, vmem],
        out_specs=vmem,
        scratch_shapes=[pltpu.VMEM((rows + 2 * capacity, width), F32)],
        compiler_params=pltpu.CompilerParams(vmem_limit_bytes=40 * MIB),
        name="cut",
    )(starts, rank, feat)
    return send, cells


def spread_cells(cells, part):
    sources = cells.shape[0]
    lane = lax.broadcasted_iota(I32, (128, 128), 1)
    pick = ones_where(
        lax.broadcasted_iota(I32, (128, 128), 0) == lane % UNIT + part * UNIT
    ).astype(BF16)
    high = dot((cells // 128).astype(F32).astype(BF16), pick)
    low = dot((cells % 128).astype(F32).astype(BF16), pick)
    value = high * 128.0 + low
    keep = lax.broadcasted_iota(I32, (sources, 128), 1) // UNIT == (
        lax.broadcasted_iota(I32, (sources, 128), 0) % 8
    )
    value = jnp.where(keep, value, 0.0).reshape(sources // 8, 8, 128)
    return jnp.sum(value, axis=1).astype(I32) - 1


def add_part(feats, spots, weight, bias, embed, total, count):
    slots = feats.shape[0]
    for block in range(slots // 512):
        at = slice(block * 512, (block + 1) * 512)
        embed[at, :] = gelu(dot(feats[at], weight[...]) + bias[...]).astype(BF16)

    def cell_block(block, _):
        first = pl.multiple_of(block * BLOCK, BLOCK)
        ids = lax.broadcasted_iota(I32, (BLOCK, 128), 0) + first
        hits = [ones_where(ids == spots[group : group + 1, :]) for group in range(slots // 128)]
        seen = hits[0]
        for hit in hits[1:]:
            seen = seen + hit
        match = jnp.concatenate([hit.astype(BF16) for hit in hits], axis=1)
        total[pl.ds(first, BLOCK), :] += dot(match, embed[...])
        count[pl.ds(first, BLOCK), :] += seen
        return 0

    lax.fori_loop(0, total.shape[0] // BLOCK, cell_block, 0)


def finish_grid(state, obs_gain, norm_gain, total, count, grid, normed):
    def block_of(block, _):
        at = pl.ds(pl.multiple_of(block * BLOCK, BLOCK), BLOCK)
        number = jnp.maximum(jnp.sum(count[at, :], axis=1, keepdims=True), 1.0)
        value = state[at, :].astype(F32) + obs_gain[...] * (total[at, :] * (1.0 / number))
        rounded = value.astype(BF16)
        grid[at, :] = rounded
        value = rounded.astype(F32)
        scale = lax.rsqrt(jnp.mean(value * value, axis=1, keepdims=True) + EPS)
        normed[at, :] = (value * scale * norm_gain[...]).astype(BF16)
        return 0

    lax.fori_loop(0, total.shape[0] // BLOCK, block_of, 0)


def assimilate_kernel(
    arrived, cells, state, weight, bias, obs_gain, norm_gain, grid, normed, embed, total, count, spots
):
    parts = arrived.shape[1]
    sources = arrived.shape[0]
    total[...] = jnp.zeros_like(total)
    count[...] = jnp.zeros_like(count)
    for part in range(parts):
        spots[part] = spread_cells(cells[...], part)

    def one(part, _):
        feats = arrived[:, part].reshape(sources * UNIT, arrived.shape[3])
        add_part(feats, spots.at[part], weight, bias, embed, total, count)
        return 0

    lax.fori_loop(0, parts, one, 0)
    finish_grid(state, obs_gain, norm_gain, total, count, grid, normed)


def assimilate(arrived, cells, state, weight, bias, obs_gain, norm_gain):
    cell_count, width = state.shape
    sources, parts = arrived.shape[:2]
    return pl.pallas_call(
        assimilate_kernel,
        out_shape=(jax.ShapeDtypeStruct(state.shape, BF16),) * 2,
        in_specs=[pl.BlockSpec(memory_space=pltpu.VMEM)] * 7,
        out_specs=[pl.BlockSpec(memory_space=pltpu.VMEM)] * 2,
        scratch_shapes=[
            pltpu.VMEM((sources * UNIT, width), BF16),
            pltpu.VMEM((cell_count, width), F32),
            pltpu.VMEM((cell_count, 128), F32),
            pltpu.VMEM((parts, sources // 8, 128), I32),
        ],
        compiler_params=pltpu.CompilerParams(vmem_limit_bytes=50 * MIB),
        name="assimilate",
    )(arrived, cells, state, weight, bias, obs_gain, norm_gain)


def halo_kernel(
    normed, north, south, seam, edges, east_block, seam_out, above, below, from_east, seam_in,
    up_sems, down_sems, east_send, east_recv, seam_send, seam_recv,
):
    faces, tiles = lax.axis_size("face"), lax.axis_size("tile")
    face, tile = lax.axis_index("face"), lax.axis_index("tile")
    cell_count, width = normed.shape
    side = above.shape[0]
    rows = cell_count // side
    following, preceding = lax.rem(face + 1, faces), lax.rem(face + faces - 1, faces)
    is_first, is_last = tile == 0, tile == tiles - 1
    barrier = pltpu.get_barrier_semaphore()

    def greet(who):
        pl.semaphore_signal(barrier, inc=1, device_id=who, device_id_type=MESH)

    greet((following, 0))

    @pl.when(jnp.logical_not(is_first))
    def _():
        greet((face, tile - 1))

    @pl.when(jnp.logical_not(is_last))
    def _():
        greet((face, tile + 1))

    @pl.when(is_first)
    def _():
        def one(other, _):
            greet((preceding, other))
            return 0

        lax.fori_loop(0, tiles, one, 0)

    edges[0] = normed[0:side, :]
    edges[1] = normed[cell_count - side : cell_count, :]
    for row in range(rows):
        last = normed[(rows - row) * side - 16 : (rows - row) * side, :].astype(F32)
        east_block[row : row + 1, :] = last[15:16, :]

    @pl.when(is_first)
    def _():
        slot = lax.broadcasted_iota(I32, (tiles * UNIT, side), 0)
        want = side - 1 - (slot // UNIT * rows - 1 + slot % UNIT)
        chosen = ones_where(lax.broadcasted_iota(I32, (tiles * UNIT, side), 1) == want)
        seam_out[...] = dot(chosen.astype(BF16), normed[0:side, :]).astype(BF16).reshape(
            tiles, UNIT, width
        )

    partners = 1 + jnp.where(is_first, tiles, 1) + jnp.where(is_last, 0, 1)
    pl.semaphore_wait(barrier, partners)

    up = pltpu.make_async_remote_copy(
        src_ref=edges.at[0], dst_ref=below,
        send_sem=up_sems.at[0], recv_sem=up_sems.at[1],
        device_id=(face, jnp.maximum(tile - 1, 0)), device_id_type=MESH,
    )
    down = pltpu.make_async_remote_copy(
        src_ref=edges.at[1], dst_ref=above,
        send_sem=down_sems.at[0], recv_sem=down_sems.at[1],
        device_id=(face, jnp.minimum(tile + 1, tiles - 1)), device_id_type=MESH,
    )
    east = pltpu.make_async_remote_copy(
        src_ref=east_block, dst_ref=from_east.at[tiles - 1 - tile],
        send_sem=east_send, recv_sem=east_recv.at[tile],
        device_id=(following, 0), device_id_type=MESH,
    )

    def seam_copy(other):
        return pltpu.make_async_remote_copy(
            src_ref=seam_out.at[other], dst_ref=seam_in,
            send_sem=seam_send.at[other], recv_sem=seam_recv,
            device_id=(preceding, other), device_id_type=MESH,
        )

    @pl.when(is_first)
    def _():
        def one(other, _):
            seam_copy(other).start()
            return 0

        lax.fori_loop(0, tiles, one, 0)

    east.start()

    @pl.when(jnp.logical_not(is_first))
    def _():
        up.start()

    @pl.when(jnp.logical_not(is_last))
    def _():
        down.start()

    @pl.when(jnp.logical_not(is_last))
    def _():
        up.wait_recv()
        south[...] = below[...]
        down.wait_send()

    @pl.when(is_last)
    def _():
        south[...] = jnp.zeros_like(south)

    @pl.when(jnp.logical_not(is_first))
    def _():
        down.wait_recv()
        north[...] = above[...]
        up.wait_send()

    east.wait_send()
    pltpu.make_async_remote_copy(
        src_ref=seam_out.at[0], dst_ref=seam_in,
        send_sem=seam_send.at[0], recv_sem=seam_recv,
        device_id=(following, 0), device_id_type=MESH,
    ).wait_recv()
    seam[...] = seam_in[...].astype(F32)

    @pl.when(is_first)
    def _():
        def one(other, _):
            seam_copy(other).wait_send()
            pltpu.make_async_remote_copy(
                src_ref=east_block, dst_ref=from_east.at[tiles - 1 - other],
                send_sem=east_send, recv_sem=east_recv.at[other],
                device_id=(preceding, other), device_id_type=MESH,
            ).wait_recv()
            return 0

        lax.fori_loop(0, tiles, one, 0)
        north[...] = from_east[...].reshape(side, width).astype(BF16)


def exchange_halo(normed, tiles, rows):
    cell_count, width = normed.shape
    side = cell_count // rows
    return pl.pallas_call(
        halo_kernel,
        out_shape=(
            jax.ShapeDtypeStruct((side, width), BF16),
            jax.ShapeDtypeStruct((side, width), BF16),
            jax.ShapeDtypeStruct((UNIT, width), F32),
        ),
        in_specs=[pl.BlockSpec(memory_space=pltpu.VMEM)],
        out_specs=[pl.BlockSpec(memory_space=pltpu.VMEM)] * 3,
        scratch_shapes=[
            pltpu.VMEM((2, side, width), BF16),
            pltpu.VMEM((rows, width), F32),
            pltpu.VMEM((tiles, UNIT, width), BF16),
            pltpu.VMEM((side, width), BF16),
            pltpu.VMEM((side, width), BF16),
            pltpu.VMEM((tiles, rows, width), F32),
            pltpu.VMEM((UNIT, width), BF16),
            pltpu.SemaphoreType.DMA((2,)),
            pltpu.SemaphoreType.DMA((2,)),
            pltpu.SemaphoreType.DMA,
            pltpu.SemaphoreType.DMA((tiles,)),
            pltpu.SemaphoreType.DMA((tiles,)),
            pltpu.SemaphoreType.DMA,
        ],
        compiler_params=pltpu.CompilerParams(
            collective_id=1, has_side_effects=True, vmem_limit_bytes=30 * MIB
        ),
        name="halo",
    )(normed)


def block_kernel(
    normed, north, south, seam, grid, conv_weight, mlp_gain, mlp_in, mlp_out, out, planes, *, per
):
    step = pl.program_id(0)
    steps = pl.num_programs(0)
    side, width = north.shape
    hidden_step = 512

    def put(row, values):
        values = values.astype(F32)
        at = lax.broadcasted_iota(I32, (side, width), 0)
        left = jnp.where(at == 0, 0.0, pltpu.roll(values, 1, 0))
        right = jnp.where(at == side - 1, seam[pl.ds(row, 1), :], pltpu.roll(values, side - 1, 0))
        planes[row, :, 0:width] = left.astype(BF16)
        planes[row, :, width : 2 * width] = values.astype(BF16)
        planes[row, :, 2 * width : 3 * width] = right.astype(BF16)

    def strip_row(row):
        return normed[pl.ds(pl.multiple_of(row * side, side), side), :]

    @pl.when(step == 0)
    def _():
        put(0, north[...])
        put(1, normed[0:side, :])

    for ahead in range(per):
        row = step * per + 2 + ahead
        if ahead < per - 1:
            put(row, strip_row(row - 1))
        else:
            inner = strip_row(jnp.minimum(row - 1, steps * per - 1))
            put(row, jnp.where(step == steps - 1, south[...], inner))

    conv = None
    for tap in range(3):
        window = planes[pl.ds(step * per + tap, per)].reshape(per * side, 3 * width)
        term = dot(window, conv_weight[tap])
        conv = term if conv is None else conv + term
    mid = grid[...].astype(F32) + conv
    scale = lax.rsqrt(jnp.mean(mid * mid, axis=1, keepdims=True) + EPS)
    normed_two = (mid * scale * mlp_gain[...]).astype(BF16)
    result = mid
    for part in range(mlp_in.shape[1] // hidden_step):
        at = slice(part * hidden_step, (part + 1) * hidden_step)
        hidden = gelu(dot(normed_two, mlp_in[:, at])).astype(BF16)
        result = result + dot(hidden, mlp_out[at, :])
    out[...] = result.astype(BF16)


def encode(normed, north, south, seam, grid, conv_weight, mlp_gain, mlp_in, mlp_out, per=2):
    cell_count, width = normed.shape
    side = north.shape[0]
    rows = cell_count // side
    whole = pl.BlockSpec(memory_space=pltpu.VMEM)
    strip = pl.BlockSpec((per * side, width), lambda i: (i, 0))

    def body(*refs):
        block_kernel(*refs, per=per)

    return pl.pallas_call(
        body,
        grid=(rows // per,),
        out_shape=jax.ShapeDtypeStruct(normed.shape, BF16),
        in_specs=[whole, whole, whole, whole, strip, whole, whole, whole, whole],
        out_specs=strip,
        scratch_shapes=[pltpu.VMEM((rows + 2, side, 3 * width), BF16)],
        compiler_params=pltpu.CompilerParams(vmem_limit_bytes=56 * MIB),
        name="encode",
    )(normed, north, south, seam, grid, conv_weight, mlp_gain, mlp_in, mlp_out)


def encode_plain(normed, north, south, seam, grid, conv_weight, mlp_gain, mlp_in, mlp_out):
    cell_count, width = normed.shape
    side = north.shape[0]
    rows = cell_count // side
    sides = jnp.concatenate([north, normed, south]).reshape(rows + 2, side, width)
    zero_col = jnp.zeros((rows + 2, 1, width), BF16)
    seam = seam[: rows + 2, None].astype(BF16)
    padded = jnp.concatenate([zero_col, sides, seam], axis=1)
    conv = jnp.zeros((cell_count, width), F32)
    for tap_row in range(3):
        for tap_col in range(3):
            window = padded[tap_row : tap_row + rows, tap_col : tap_col + side].reshape(-1, width)
            conv = conv + dot(window, conv_weight[3 * tap_row + tap_col])
    mid = grid.astype(F32) + conv
    scale = lax.rsqrt(jnp.mean(mid * mid, axis=-1, keepdims=True) + EPS)
    normed_two = (mid * scale * mlp_gain).astype(BF16)
    hidden = jax.nn.gelu(dot(normed_two, mlp_in)).astype(BF16)
    return (mid + dot(hidden, mlp_out)).astype(BF16)


def shards(
    state,
    obs_feat,
    obs_dest,
    obs_cell,
    obs_weight,
    obs_bias,
    obs_gain,
    norm_gain,
    conv_weight,
    mlp_gain,
    mlp_in,
    mlp_out,
):
    tiles = lax.axis_size("tile")
    devices = lax.axis_size("face") * tiles
    held = obs_feat.shape[0]
    capacity = 4 * held // devices
    rows, side, width = state.shape[2:]
    send, cells = pack(
        obs_dest.reshape(1, held), obs_cell.reshape(1, held), obs_feat, devices, capacity
    )
    arrived = lax.all_to_all(send, ("face", "tile"), split_axis=0, concat_axis=0, tiled=True)
    cells = lax.all_to_all(cells, ("face", "tile"), split_axis=0, concat_axis=0, tiled=True)
    grid, normed = assimilate(
        arrived,
        cells,
        state.reshape(rows * side, width),
        obs_weight,
        obs_bias.reshape(1, width),
        obs_gain.reshape(1, width),
        norm_gain.reshape(1, width),
    )
    north, south, seam = exchange_halo(normed, tiles, rows)
    result = encode_plain(
        normed,
        north,
        south,
        seam,
        grid,
        conv_weight,
        mlp_gain.reshape(1, width),
        mlp_in,
        mlp_out,
    )
    return result.reshape(state.shape)


def solution(mesh):
    placed = (
        P("face", "tile", None, None, None),
        P(("face", "tile"), None),
        P(("face", "tile"), None),
        P(("face", "tile")),
    ) + (P(),) * 8
    return jax.shard_map(
        shards,
        mesh=mesh,
        in_specs=placed,
        out_specs=P("face", "tile", None, None, None),
        check_vma=False,
    )
```

```python
import math

import jax
import jax.numpy as jnp
from jax import lax
from jax.experimental import pallas as pl
from jax.experimental.pallas import tpu as pltpu
from jax.sharding import PartitionSpec as P

BF16 = jnp.bfloat16
F32 = jnp.float32
I32 = jnp.int32
MESH = pl.DeviceIdType.MESH
EPS = 1e-05
MIB = 2**20
UNIT = 16
BLOCK = 256


def gelu(x):
    inner = x * (math.sqrt(2.0 / math.pi) + (0.044715 * math.sqrt(2.0 / math.pi)) * (x * x))
    half = 0.5 * x
    return half + half * jnp.tanh(inner)


def ones_where(mask):
    return jnp.where(mask, 1.0, 0.0)


def dot(a, b):
    return jnp.dot(a, b, preferred_element_type=F32)


def dot_lanes(a, b):
    return lax.dot_general(a, b, (((1,), (1,)), ((), ())), preferred_element_type=F32)


def rank_kernel(dest, cell, rank, starts, cells):
    devices = starts.shape[1]
    rows = dest.shape[1]
    hot = lax.broadcasted_iota(I32, (devices, rows), 0) == dest[...]
    hot_f = ones_where(hot)
    hot_b = hot_f.astype(BF16)
    before = ones_where(
        lax.broadcasted_iota(I32, (BLOCK, BLOCK), 0) < lax.broadcasted_iota(I32, (BLOCK, BLOCK), 1)
    ).astype(BF16)
    ahead = jnp.zeros((devices, 1), F32)
    pieces = []
    for block in range(rows // BLOCK):
        at = slice(block * BLOCK, (block + 1) * BLOCK)
        pieces.append(dot(hot_b[:, at], before) + ahead)
        ahead = ahead + jnp.sum(hot_f[:, at], axis=1, keepdims=True)
    earlier = jnp.concatenate(pieces, axis=1)
    row_id = lax.broadcasted_iota(I32, (devices, devices), 0)
    col_id = lax.broadcasted_iota(I32, (devices, devices), 1)
    start = dot(
        ones_where(col_id < row_id).astype(BF16),
        jnp.broadcast_to(ahead, (devices, devices)).astype(BF16),
    )
    starts[...] = jnp.sum(jnp.where(row_id == col_id, start, 0.0), axis=0, keepdims=True).astype(I32)
    rank_in = jnp.sum(hot_f * earlier, axis=0, keepdims=True).astype(I32)
    rank[...] = jnp.sum(hot_f * (earlier + start[:, :1]), axis=0, keepdims=True).astype(I32)
    spot = cell[...] + 1
    high = hot_f * (spot // 128).astype(F32)
    low = hot_f * (spot % 128).astype(F32)
    in_slot = ones_where(lax.broadcasted_iota(I32, (128, rows), 0) == rank_in).astype(BF16)
    split = dot_lanes(jnp.concatenate([high, low], axis=0).astype(BF16), in_slot)
    cells[...] = (split[:devices] * 128.0 + split[devices:]).astype(I32)


def cut_kernel(starts, rank, feat, send, ordered):
    devices = send.shape[0]
    rows = feat.shape[0]
    capacity = send.shape[1] * send.shape[2]

    def sort_block(block, _):
        first = pl.multiple_of(block * BLOCK, BLOCK)
        chosen = ones_where(
            lax.broadcasted_iota(I32, (BLOCK, rows), 0) + first == rank[...]
        ).astype(BF16)
        ordered[pl.ds(first, BLOCK), :] = dot(chosen, feat[...])
        return 0

    lax.fori_loop(0, rows // BLOCK, sort_block, 0)
    ordered[rows:, :] = jnp.zeros((ordered.shape[0] - rows, feat.shape[1]), F32)

    def cut(target, _):
        values = ordered[pl.ds(starts[0, target], capacity), :]
        send[target] = values.astype(BF16).reshape(send.shape[1:])
        return 0

    lax.fori_loop(0, devices, cut, 0, unroll=4)


def pack(dest, cell, feat, devices, capacity):
    rows, width = feat.shape
    vmem = pl.BlockSpec(memory_space=pltpu.VMEM)
    rank, starts, cells = pl.pallas_call(
        rank_kernel,
        out_shape=(
            jax.ShapeDtypeStruct((1, rows), I32),
            jax.ShapeDtypeStruct((1, devices), I32),
            jax.ShapeDtypeStruct((devices, 128), I32),
        ),
        in_specs=[vmem] * 2,
        out_specs=[vmem] * 3,
        compiler_params=pltpu.CompilerParams(vmem_limit_bytes=16 * MIB),
        name="rank",
    )(dest, cell)
    send = pl.pallas_call(
        cut_kernel,
        out_shape=jax.ShapeDtypeStruct((devices, capacity // UNIT, UNIT, width), BF16),
        in_specs=[pl.BlockSpec(memory_space=pltpu.SMEM), vmem, vmem],
        out_specs=vmem,
        scratch_shapes=[pltpu.VMEM((rows + 2 * capacity, width), F32)],
        compiler_params=pltpu.CompilerParams(vmem_limit_bytes=16 * MIB),
        name="cut",
    )(starts, rank, feat)
    return send, cells


def spread_cells(cells, part):
    sources = cells.shape[0]
    lane = lax.broadcasted_iota(I32, (128, 128), 1)
    pick = ones_where(
        lax.broadcasted_iota(I32, (128, 128), 0) == lane % UNIT + part * UNIT
    ).astype(BF16)
    high = dot((cells // 128).astype(F32).astype(BF16), pick)
    low = dot((cells % 128).astype(F32).astype(BF16), pick)
    value = high * 128.0 + low
    keep = lax.broadcasted_iota(I32, (sources, 128), 1) // UNIT == (
        lax.broadcasted_iota(I32, (sources, 128), 0) % 8
    )
    value = jnp.where(keep, value, 0.0).reshape(sources // 8, 8, 128)
    return jnp.sum(value, axis=1).astype(I32) - 1


def add_part(feats, spots, weight, bias, embed, total, count):
    slots = feats.shape[0]
    for block in range(slots // 512):
        at = slice(block * 512, (block + 1) * 512)
        embed[at, :] = gelu(dot(feats[at], weight[...]) + bias[...]).astype(BF16)

    def cell_block(block, _):
        first = pl.multiple_of(block * BLOCK, BLOCK)
        ids = lax.broadcasted_iota(I32, (BLOCK, 128), 0) + first
        hits = [ones_where(ids == spots[group : group + 1, :]) for group in range(slots // 128)]
        seen = hits[0]
        for hit in hits[1:]:
            seen = seen + hit
        match = jnp.concatenate([hit.astype(BF16) for hit in hits], axis=1)
        total[pl.ds(first, BLOCK), :] += dot(match, embed[...])
        count[pl.ds(first, BLOCK), :] += seen
        return 0

    lax.fori_loop(0, total.shape[0] // BLOCK, cell_block, 0)


def finish_grid(state, obs_gain, norm_gain, total, count, grid, normed):
    def block_of(block, _):
        at = pl.ds(pl.multiple_of(block * BLOCK, BLOCK), BLOCK)
        number = jnp.maximum(jnp.sum(count[at, :], axis=1, keepdims=True), 1.0)
        value = state[at, :].astype(F32) + obs_gain[...] * (total[at, :] * (1.0 / number))
        rounded = value.astype(BF16)
        grid[at, :] = rounded
        value = rounded.astype(F32)
        scale = lax.rsqrt(jnp.mean(value * value, axis=1, keepdims=True) + EPS)
        normed[at, :] = (value * scale * norm_gain[...]).astype(BF16)
        return 0

    lax.fori_loop(0, total.shape[0] // BLOCK, block_of, 0)


def assimilate_kernel(
    arrived, cells, state, weight, bias, obs_gain, norm_gain, grid, normed, embed, total, count, spots
):
    parts = arrived.shape[1]
    sources = arrived.shape[0]
    total[...] = jnp.zeros_like(total)
    count[...] = jnp.zeros_like(count)
    for part in range(parts):
        spots[part] = spread_cells(cells[...], part)

    def one(part, _):
        feats = arrived[:, part].reshape(sources * UNIT, arrived.shape[3])
        add_part(feats, spots.at[part], weight, bias, embed, total, count)
        return 0

    lax.fori_loop(0, parts, one, 0)
    finish_grid(state, obs_gain, norm_gain, total, count, grid, normed)


def assimilate(arrived, cells, state, weight, bias, obs_gain, norm_gain):
    cell_count, width = state.shape
    sources, parts = arrived.shape[:2]
    return pl.pallas_call(
        assimilate_kernel,
        out_shape=(jax.ShapeDtypeStruct(state.shape, BF16),) * 2,
        in_specs=[pl.BlockSpec(memory_space=pltpu.VMEM)] * 7,
        out_specs=[pl.BlockSpec(memory_space=pltpu.VMEM)] * 2,
        scratch_shapes=[
            pltpu.VMEM((sources * UNIT, width), BF16),
            pltpu.VMEM((cell_count, width), F32),
            pltpu.VMEM((cell_count, 128), F32),
            pltpu.VMEM((parts, sources // 8, 128), I32),
        ],
        compiler_params=pltpu.CompilerParams(vmem_limit_bytes=24 * MIB),
        name="assimilate",
    )(arrived, cells, state, weight, bias, obs_gain, norm_gain)


def halo_kernel(
    normed, north, south, seam, edges, east_block, seam_out, above, below, from_east, seam_in,
    up_sems, down_sems, east_send, east_recv, seam_send, seam_recv,
):
    faces, tiles = lax.axis_size("face"), lax.axis_size("tile")
    face, tile = lax.axis_index("face"), lax.axis_index("tile")
    cell_count, width = normed.shape
    side = above.shape[0]
    rows = cell_count // side
    following, preceding = lax.rem(face + 1, faces), lax.rem(face + faces - 1, faces)
    is_first, is_last = tile == 0, tile == tiles - 1
    barrier = pltpu.get_barrier_semaphore()

    def greet(who):
        pl.semaphore_signal(barrier, inc=1, device_id=who, device_id_type=MESH)

    greet((following, 0))

    @pl.when(jnp.logical_not(is_first))
    def _():
        greet((face, tile - 1))

    @pl.when(jnp.logical_not(is_last))
    def _():
        greet((face, tile + 1))

    @pl.when(is_first)
    def _():
        def one(other, _):
            greet((preceding, other))
            return 0

        lax.fori_loop(0, tiles, one, 0)

    edges[0] = normed[0:side, :]
    edges[1] = normed[cell_count - side : cell_count, :]
    for row in range(rows):
        last = normed[(rows - row) * side - 16 : (rows - row) * side, :].astype(F32)
        east_block[row : row + 1, :] = last[15:16, :]

    @pl.when(is_first)
    def _():
        slot = lax.broadcasted_iota(I32, (tiles * UNIT, side), 0)
        want = side - 1 - (slot // UNIT * rows - 1 + slot % UNIT)
        chosen = ones_where(lax.broadcasted_iota(I32, (tiles * UNIT, side), 1) == want)
        seam_out[...] = dot(chosen.astype(BF16), normed[0:side, :]).astype(BF16).reshape(
            tiles, UNIT, width
        )

    partners = 1 + jnp.where(is_first, tiles, 1) + jnp.where(is_last, 0, 1)
    pl.semaphore_wait(barrier, partners)

    up = pltpu.make_async_remote_copy(
        src_ref=edges.at[0], dst_ref=below,
        send_sem=up_sems.at[0], recv_sem=up_sems.at[1],
        device_id=(face, jnp.maximum(tile - 1, 0)), device_id_type=MESH,
    )
    down = pltpu.make_async_remote_copy(
        src_ref=edges.at[1], dst_ref=above,
        send_sem=down_sems.at[0], recv_sem=down_sems.at[1],
        device_id=(face, jnp.minimum(tile + 1, tiles - 1)), device_id_type=MESH,
    )
    east = pltpu.make_async_remote_copy(
        src_ref=east_block, dst_ref=from_east.at[tiles - 1 - tile],
        send_sem=east_send, recv_sem=east_recv.at[tile],
        device_id=(following, 0), device_id_type=MESH,
    )

    def seam_copy(other):
        return pltpu.make_async_remote_copy(
            src_ref=seam_out.at[other], dst_ref=seam_in,
            send_sem=seam_send.at[other], recv_sem=seam_recv,
            device_id=(preceding, other), device_id_type=MESH,
        )

    @pl.when(is_first)
    def _():
        def one(other, _):
            seam_copy(other).start()
            return 0

        lax.fori_loop(0, tiles, one, 0)

    east.start()

    @pl.when(jnp.logical_not(is_first))
    def _():
        up.start()

    @pl.when(jnp.logical_not(is_last))
    def _():
        down.start()

    @pl.when(jnp.logical_not(is_last))
    def _():
        up.wait_recv()
        south[...] = below[...]
        down.wait_send()

    @pl.when(is_last)
    def _():
        south[...] = jnp.zeros_like(south)

    @pl.when(jnp.logical_not(is_first))
    def _():
        down.wait_recv()
        north[...] = above[...]
        up.wait_send()

    east.wait_send()
    pltpu.make_async_remote_copy(
        src_ref=seam_out.at[0], dst_ref=seam_in,
        send_sem=seam_send.at[0], recv_sem=seam_recv,
        device_id=(following, 0), device_id_type=MESH,
    ).wait_recv()
    seam[...] = seam_in[...].astype(F32)

    @pl.when(is_first)
    def _():
        def one(other, _):
            seam_copy(other).wait_send()
            pltpu.make_async_remote_copy(
                src_ref=east_block, dst_ref=from_east.at[tiles - 1 - other],
                send_sem=east_send, recv_sem=east_recv.at[other],
                device_id=(preceding, other), device_id_type=MESH,
            ).wait_recv()
            return 0

        lax.fori_loop(0, tiles, one, 0)
        north[...] = from_east[...].reshape(side, width).astype(BF16)


def exchange_halo(normed, tiles, rows):
    cell_count, width = normed.shape
    side = cell_count // rows
    return pl.pallas_call(
        halo_kernel,
        out_shape=(
            jax.ShapeDtypeStruct((side, width), BF16),
            jax.ShapeDtypeStruct((side, width), BF16),
            jax.ShapeDtypeStruct((UNIT, width), F32),
        ),
        in_specs=[pl.BlockSpec(memory_space=pltpu.VMEM)],
        out_specs=[pl.BlockSpec(memory_space=pltpu.VMEM)] * 3,
        scratch_shapes=[
            pltpu.VMEM((2, side, width), BF16),
            pltpu.VMEM((rows, width), F32),
            pltpu.VMEM((tiles, UNIT, width), BF16),
            pltpu.VMEM((side, width), BF16),
            pltpu.VMEM((side, width), BF16),
            pltpu.VMEM((tiles, rows, width), F32),
            pltpu.VMEM((UNIT, width), BF16),
            pltpu.SemaphoreType.DMA((2,)),
            pltpu.SemaphoreType.DMA((2,)),
            pltpu.SemaphoreType.DMA,
            pltpu.SemaphoreType.DMA((tiles,)),
            pltpu.SemaphoreType.DMA((tiles,)),
            pltpu.SemaphoreType.DMA,
        ],
        compiler_params=pltpu.CompilerParams(
            collective_id=1, has_side_effects=True, vmem_limit_bytes=16 * MIB
        ),
        name="halo",
    )(normed)


def encode_kernel(
    normed, north, south, seam, grid, conv_weight, mlp_gain, mlp_in, mlp_out, out, planes
):
    side, width = north.shape
    cells = normed.shape[0]
    rows = cells // side
    per = 2
    hidden_step = 512

    def put(row, values):
        values = values.astype(F32)
        at = lax.broadcasted_iota(I32, (side, width), 0)
        left = jnp.where(at == 0, 0.0, pltpu.roll(values, 1, 0))
        right = jnp.where(at == side - 1, seam[pl.ds(row, 1), :], pltpu.roll(values, side - 1, 0))
        to = pl.ds(pl.multiple_of(row * side, side), side)
        planes[to, 0:width] = left.astype(BF16)
        planes[to, width : 2 * width] = values.astype(BF16)
        planes[to, 2 * width : 3 * width] = right.astype(BF16)

    put(0, north[...])
    put(rows + 1, south[...])

    def inner(row, _):
        put(row + 1, normed[pl.ds(pl.multiple_of(row * side, side), side), :])
        return 0

    lax.fori_loop(0, rows, inner, 0)

    def one(step, _):
        first = pl.multiple_of(step * (per * side), per * side)
        conv = None
        for tap in range(3):
            window = planes[pl.ds(pl.multiple_of(first + tap * side, side), per * side), :]
            term = dot(window, conv_weight[tap])
            conv = term if conv is None else conv + term
        mid = grid[pl.ds(first, per * side), :].astype(F32) + conv
        scale = lax.rsqrt(jnp.mean(mid * mid, axis=1, keepdims=True) + EPS)
        normed_two = (mid * scale * mlp_gain[...]).astype(BF16)
        result = mid
        for part in range(mlp_in.shape[1] // hidden_step):
            at = slice(part * hidden_step, (part + 1) * hidden_step)
            hidden = gelu(dot(normed_two, mlp_in[:, at])).astype(BF16)
            result = result + dot(hidden, mlp_out[at, :])
        out[pl.ds(first, per * side), :] = result.astype(BF16)
        return 0

    lax.fori_loop(0, rows // per, one, 0)


def encode(normed, north, south, seam, grid, conv_weight, mlp_gain, mlp_in, mlp_out):
    cell_count, width = normed.shape
    side = north.shape[0]
    vmem = pl.BlockSpec(memory_space=pltpu.VMEM)
    return pl.pallas_call(
        encode_kernel,
        out_shape=jax.ShapeDtypeStruct(normed.shape, BF16),
        in_specs=[vmem] * 9,
        out_specs=vmem,
        scratch_shapes=[pltpu.VMEM((cell_count + 2 * side, 3 * width), BF16)],
        compiler_params=pltpu.CompilerParams(vmem_limit_bytes=40 * MIB),
        name="encode",
    )(normed, north, south, seam, grid, conv_weight, mlp_gain, mlp_in, mlp_out)


def shards(
    state,
    obs_feat,
    obs_dest,
    obs_cell,
    obs_weight,
    obs_bias,
    obs_gain,
    norm_gain,
    conv_weight,
    mlp_gain,
    mlp_in,
    mlp_out,
):
    tiles = lax.axis_size("tile")
    devices = lax.axis_size("face") * tiles
    held = obs_feat.shape[0]
    capacity = 4 * held // devices
    rows, side, width = state.shape[2:]
    send, cells = pack(
        obs_dest.reshape(1, held), obs_cell.reshape(1, held), obs_feat, devices, capacity
    )
    arrived = lax.all_to_all(send, ("face", "tile"), split_axis=0, concat_axis=0, tiled=True)
    cells = lax.all_to_all(cells, ("face", "tile"), split_axis=0, concat_axis=0, tiled=True)
    grid, normed = assimilate(
        arrived,
        cells,
        state.reshape(rows * side, width),
        obs_weight,
        obs_bias.reshape(1, width),
        obs_gain.reshape(1, width),
        norm_gain.reshape(1, width),
    )
    north, south, seam = exchange_halo(normed, tiles, rows)
    result = encode(
        normed,
        north,
        south,
        seam,
        grid,
        conv_weight.reshape(3, 3 * width, width),
        mlp_gain.reshape(1, width),
        mlp_in,
        mlp_out,
    )
    return result.reshape(state.shape)


def solution(mesh):
    placed = (
        P("face", "tile", None, None, None),
        P(("face", "tile"), None),
        P(("face", "tile"), None),
        P(("face", "tile")),
    ) + (P(),) * 8
    return jax.shard_map(
        shards,
        mesh=mesh,
        in_specs=placed,
        out_specs=P("face", "tile", None, None, None),
        check_vma=False,
    )
```

```python
import math

import jax
import jax.numpy as jnp
from jax import lax
from jax.experimental import pallas as pl
from jax.experimental.pallas import tpu as pltpu
from jax.sharding import PartitionSpec as P

BF16 = jnp.bfloat16
F32 = jnp.float32
I32 = jnp.int32
MESH = pl.DeviceIdType.MESH
EPS = 1e-05
MIB = 2**20
UNIT = 16
BLOCK = 256


def gelu(x):
    inner = x * (math.sqrt(2.0 / math.pi) + (0.044715 * math.sqrt(2.0 / math.pi)) * (x * x))
    half = 0.5 * x
    return half + half * jnp.tanh(inner)


def ones_where(mask):
    return jnp.where(mask, 1.0, 0.0)


def dot(a, b):
    return jnp.dot(a, b, preferred_element_type=F32)


def dot_lanes(a, b):
    return lax.dot_general(a, b, (((1,), (1,)), ((), ())), preferred_element_type=F32)


def rank_kernel(dest, cell, rank, starts, cells):
    devices = starts.shape[1]
    rows = dest.shape[1]
    hot = lax.broadcasted_iota(I32, (devices, rows), 0) == dest[...]
    hot_f = ones_where(hot)
    hot_b = hot_f.astype(BF16)
    before = ones_where(
        lax.broadcasted_iota(I32, (BLOCK, BLOCK), 0) < lax.broadcasted_iota(I32, (BLOCK, BLOCK), 1)
    ).astype(BF16)
    ahead = jnp.zeros((devices, 1), F32)
    pieces = []
    for block in range(rows // BLOCK):
        at = slice(block * BLOCK, (block + 1) * BLOCK)
        pieces.append(dot(hot_b[:, at], before) + ahead)
        ahead = ahead + jnp.sum(hot_f[:, at], axis=1, keepdims=True)
    earlier = jnp.concatenate(pieces, axis=1)
    row_id = lax.broadcasted_iota(I32, (devices, devices), 0)
    col_id = lax.broadcasted_iota(I32, (devices, devices), 1)
    start = dot(
        ones_where(col_id < row_id).astype(BF16),
        jnp.broadcast_to(ahead, (devices, devices)).astype(BF16),
    )
    starts[...] = jnp.sum(jnp.where(row_id == col_id, start, 0.0), axis=0, keepdims=True).astype(I32)
    rank_in = jnp.sum(hot_f * earlier, axis=0, keepdims=True).astype(I32)
    rank[...] = jnp.sum(hot_f * (earlier + start[:, :1]), axis=0, keepdims=True).astype(I32)
    spot = cell[...] + 1
    high = hot_f * (spot // 128).astype(F32)
    low = hot_f * (spot % 128).astype(F32)
    in_slot = ones_where(lax.broadcasted_iota(I32, (128, rows), 0) == rank_in).astype(BF16)
    split = dot_lanes(jnp.concatenate([high, low], axis=0).astype(BF16), in_slot)
    cells[...] = (split[:devices] * 128.0 + split[devices:]).astype(I32)


def cut_kernel(starts, rank, feat, send, ordered):
    parts, devices = send.shape[:2]
    rows = feat.shape[0]
    capacity = parts * UNIT

    def sort_block(block, _):
        first = pl.multiple_of(block * BLOCK, BLOCK)
        chosen = ones_where(
            lax.broadcasted_iota(I32, (BLOCK, rows), 0) + first == rank[...]
        ).astype(BF16)
        ordered[pl.ds(first, BLOCK), :] = dot(chosen, feat[...])
        return 0

    lax.fori_loop(0, rows // BLOCK, sort_block, 0)
    ordered[rows:, :] = jnp.zeros((ordered.shape[0] - rows, feat.shape[1]), F32)

    def cut(target, _):
        values = ordered[pl.ds(starts[0, target], capacity), :]
        values = values.astype(BF16)
        for part in range(parts):
            send[part, target] = values[part * UNIT : (part + 1) * UNIT]
        return 0

    lax.fori_loop(0, devices, cut, 0, unroll=4)


def pack(dest, cell, feat, devices, capacity):
    rows, width = feat.shape
    vmem = pl.BlockSpec(memory_space=pltpu.VMEM)
    rank, starts, cells = pl.pallas_call(
        rank_kernel,
        out_shape=(
            jax.ShapeDtypeStruct((1, rows), I32),
            jax.ShapeDtypeStruct((1, devices), I32),
            jax.ShapeDtypeStruct((devices, 128), I32),
        ),
        in_specs=[vmem] * 2,
        out_specs=[vmem] * 3,
        compiler_params=pltpu.CompilerParams(vmem_limit_bytes=16 * MIB),
        name="rank",
    )(dest, cell)
    send = pl.pallas_call(
        cut_kernel,
        out_shape=jax.ShapeDtypeStruct((capacity // UNIT, devices, UNIT, width), BF16),
        in_specs=[pl.BlockSpec(memory_space=pltpu.SMEM), vmem, vmem],
        out_specs=vmem,
        scratch_shapes=[pltpu.VMEM((rows + 2 * capacity, width), F32)],
        compiler_params=pltpu.CompilerParams(vmem_limit_bytes=16 * MIB),
        name="cut",
    )(starts, rank, feat)
    return send, cells


def spread_cells(cells, part):
    sources = cells.shape[0]
    lane = lax.broadcasted_iota(I32, (128, 128), 1)
    pick = ones_where(
        lax.broadcasted_iota(I32, (128, 128), 0) == lane % UNIT + part * UNIT
    ).astype(BF16)
    high = dot((cells // 128).astype(F32).astype(BF16), pick)
    low = dot((cells % 128).astype(F32).astype(BF16), pick)
    value = high * 128.0 + low
    keep = lax.broadcasted_iota(I32, (sources, 128), 1) // UNIT == (
        lax.broadcasted_iota(I32, (sources, 128), 0) % 8
    )
    value = jnp.where(keep, value, 0.0).reshape(sources // 8, 8, 128)
    return jnp.sum(value, axis=1).astype(I32) - 1


def match_rows(ids, row):
    wide = jnp.broadcast_to(row, (UNIT, 128)).astype(BF16)
    wide = jnp.concatenate([wide] * (128 // UNIT), axis=0)
    return jnp.where(ids == wide, jnp.ones_like(ids), jnp.zeros_like(ids))


def add_part(feats, spots, weight, bias, embed, total, count):
    slots = feats.shape[0]
    for block in range(slots // 512):
        at = slice(block * 512, (block + 1) * 512)
        embed[at, :] = gelu(dot(feats[at], weight[...]) + bias[...]).astype(BF16)
    groups = slots // 128
    ids = lax.broadcasted_iota(I32, (128, 128), 0).astype(F32).astype(BF16)
    spot = spots[...]
    high = lax.shift_right_arithmetic(spot, 7)
    low = jnp.where(spot < 0, -1, spot - high * 128).astype(F32)
    high_f = high.astype(F32)

    def matches(rows):
        return jnp.concatenate(
            [match_rows(ids, rows[group : group + 1, :]) for group in range(groups)], axis=1
        )

    count[...] += dot_lanes(matches(low), matches(high_f))
    per = 4

    def cell_block(block, _):
        match = jnp.concatenate(
            [matches(jnp.where(high == block * per + part, low, -1.0)) for part in range(per)],
            axis=0,
        )
        at = pl.ds(pl.multiple_of(block * (per * 128), per * 128), per * 128)
        total[at, :] += dot(match, embed[...])
        return 0

    lax.fori_loop(0, total.shape[0] // (per * 128), cell_block, 0)


def finish_grid(state, obs_gain, norm_gain, total, count, grid, normed):
    lane = lax.broadcasted_iota(I32, count.shape, 1)

    def block_of(block, _):
        at = pl.ds(pl.multiple_of(block * 128, 128), 128)
        number = jnp.sum(jnp.where(lane == block, count[...], 0.0), axis=1, keepdims=True)
        number = jnp.maximum(number, 1.0)
        value = state[at, :].astype(F32) + obs_gain[...] * (total[at, :] * (1.0 / number))
        rounded = value.astype(BF16)
        grid[at, :] = rounded
        value = rounded.astype(F32)
        scale = lax.rsqrt(jnp.mean(value * value, axis=1, keepdims=True) + EPS)
        normed[at, :] = (value * scale * norm_gain[...]).astype(BF16)
        return 0

    lax.fori_loop(0, total.shape[0] // 128, block_of, 0)


def gather_kernel(
    send, cells, state, weight, bias, obs_gain, norm_gain, grid, normed,
    held, cell_held, cell_flat, spots, embed, total, count,
    send_sems, recv_sems, own_sems,
):
    parts = send.shape[0]
    face, tile = lax.axis_index("face"), lax.axis_index("tile")
    sizes = send.shape[1:4]
    mine = (face, tile // sizes[2], lax.rem(tile, sizes[2]))
    barrier = pltpu.get_barrier_semaphore()

    def other(dim, step):
        place = list(mine)
        place[dim] = lax.rem(mine[dim] + step, sizes[dim])
        return place[dim], (place[0], place[1] * sizes[2] + place[2])

    for dim in range(3):
        def greet(step, _, dim=dim):
            pl.semaphore_signal(
                barrier, inc=1, device_id=other(dim, step)[1], device_id_type=MESH
            )
            return 0

        lax.fori_loop(1, sizes[dim], greet, 0)

    def dim_of(part, stage):
        return (part + stage) % 3

    def views(part, stage):
        if part == parts:
            source = cells if stage == 0 else cell_held.at[stage - 1]
            return source, cell_held.at[stage]
        source = send.at[part] if stage == 0 else held.at[stage - 1, part]
        return source, held.at[stage, part]

    def along(ref, dim, place):
        return ref.at[(slice(None),) * dim + (place,)]

    def copies(part, stage, step):
        dim = dim_of(part, stage)
        source, target = views(part, stage)
        place, device = other(dim, step)
        return pltpu.make_async_remote_copy(
            src_ref=along(source, dim, place),
            dst_ref=along(target, dim, mine[dim]),
            send_sem=send_sems.at[part * 3 + stage, step],
            recv_sem=recv_sems.at[part * 3 + stage, step],
            device_id=device,
            device_id_type=MESH,
        )

    def own(part, stage):
        dim = dim_of(part, stage)
        source, target = views(part, stage)
        return pltpu.make_async_copy(
            along(source, dim, mine[dim]), along(target, dim, mine[dim]),
            own_sems.at[part * 3 + stage],
        )

    def start(part, stage):
        def one(step, _):
            copies(part, stage, step).start()
            return 0

        lax.fori_loop(1, sizes[dim_of(part, stage)], one, 0)
        own(part, stage).start()

    def finish(part, stage):
        def one(step, _):
            copies(part, stage, step).wait()
            return 0

        own(part, stage).wait()
        lax.fori_loop(1, sizes[dim_of(part, stage)], one, 0)

    def advance(which, stage):
        for part in which:
            finish(part, stage)
            start(part, stage + 1)

    def add(part, _=None):
        feats = held[2, part].reshape(-1, send.shape[-1])
        add_part(feats, spots.at[part], weight, bias, embed, total, count)
        return 0

    early, late = list(range(parts // 2)), list(range(parts // 2, parts))
    pl.semaphore_wait(barrier, sum(sizes) - 3)
    start(parts, 0)
    for part in early:
        start(part, 0)
    for part in late:
        start(part, 0)
    total[...] = jnp.zeros_like(total)
    count[...] = jnp.zeros_like(count)
    advance([parts], 0)
    advance(early, 0)
    advance([parts], 1)
    advance(early, 1)
    advance(late, 0)
    finish(parts, 2)

    def lay(row, _):
        across = sizes[1] * sizes[2]
        cell_flat[pl.ds(row, 1), :] = cell_held[
            2, row // across, lax.rem(row, across) // sizes[2], lax.rem(row, sizes[2])
        ]
        return 0

    lax.fori_loop(0, cell_flat.shape[0], lay, 0)
    for part in range(parts):
        spots[part] = spread_cells(cell_flat[...], part)
    finish(early[0], 2)
    add(early[0])
    advance(late, 1)
    for part in early[1:]:
        finish(part, 2)
    lax.fori_loop(early[1], early[-1] + 1, add, 0)
    for part in late:
        finish(part, 2)
    lax.fori_loop(late[0], late[-1] + 1, add, 0)
    finish_grid(state, obs_gain, norm_gain, total, count, grid, normed)


def assimilate(send, cells, state, weight, bias, obs_gain, norm_gain):
    cell_count, width = state.shape
    parts = send.shape[0]
    sources = cells.shape[0] * cells.shape[1] * cells.shape[2]
    vmem = pl.BlockSpec(memory_space=pltpu.VMEM)
    longest = max(send.shape[1:4])
    return pl.pallas_call(
        gather_kernel,
        out_shape=(jax.ShapeDtypeStruct(state.shape, BF16),) * 2,
        in_specs=[vmem] * 7,
        out_specs=[vmem] * 2,
        scratch_shapes=[
            pltpu.VMEM((3,) + send.shape, BF16),
            pltpu.VMEM((3,) + cells.shape, I32),
            pltpu.VMEM((sources, 128), I32),
            pltpu.VMEM((parts, sources // 8, 128), I32),
            pltpu.VMEM((sources * UNIT, width), BF16),
            pltpu.VMEM((cell_count, width), F32),
            pltpu.VMEM((128, 128), F32),
            pltpu.SemaphoreType.DMA((parts * 3 + 3, longest)),
            pltpu.SemaphoreType.DMA((parts * 3 + 3, longest)),
            pltpu.SemaphoreType.DMA((parts * 3 + 3,)),
        ],
        compiler_params=pltpu.CompilerParams(
            collective_id=0, has_side_effects=True, vmem_limit_bytes=34 * MIB
        ),
        name="gather",
    )(send, cells, state, weight, bias, obs_gain, norm_gain)


def halo_kernel(
    normed, north, south, seam, edges, east_block, seam_out, above, below, from_east, seam_in,
    up_sems, down_sems, east_send, east_recv, seam_send, seam_recv,
):
    faces, tiles = lax.axis_size("face"), lax.axis_size("tile")
    face, tile = lax.axis_index("face"), lax.axis_index("tile")
    cell_count, width = normed.shape
    side = above.shape[0]
    rows = cell_count // side
    following, preceding = lax.rem(face + 1, faces), lax.rem(face + faces - 1, faces)
    is_first, is_last = tile == 0, tile == tiles - 1
    barrier = pltpu.get_barrier_semaphore()

    def greet(who):
        pl.semaphore_signal(barrier, inc=1, device_id=who, device_id_type=MESH)

    greet((following, 0))

    @pl.when(jnp.logical_not(is_first))
    def _():
        greet((face, tile - 1))

    @pl.when(jnp.logical_not(is_last))
    def _():
        greet((face, tile + 1))

    @pl.when(is_first)
    def _():
        def one(other, _):
            greet((preceding, other))
            return 0

        lax.fori_loop(0, tiles, one, 0)

    edges[0] = normed[0:side, :]
    edges[1] = normed[cell_count - side : cell_count, :]
    for row in range(rows):
        last = normed[(rows - row) * side - 16 : (rows - row) * side, :].astype(F32)
        east_block[row : row + 1, :] = last[15:16, :]

    @pl.when(is_first)
    def _():
        slot = lax.broadcasted_iota(I32, (tiles * UNIT, side), 0)
        want = side - 1 - (slot // UNIT * rows - 1 + slot % UNIT)
        chosen = ones_where(lax.broadcasted_iota(I32, (tiles * UNIT, side), 1) == want)
        seam_out[...] = dot(chosen.astype(BF16), normed[0:side, :]).astype(BF16).reshape(
            tiles, UNIT, width
        )

    partners = 1 + jnp.where(is_first, tiles, 1) + jnp.where(is_last, 0, 1)
    pl.semaphore_wait(barrier, partners)

    up = pltpu.make_async_remote_copy(
        src_ref=edges.at[0], dst_ref=below,
        send_sem=up_sems.at[0], recv_sem=up_sems.at[1],
        device_id=(face, jnp.maximum(tile - 1, 0)), device_id_type=MESH,
    )
    down = pltpu.make_async_remote_copy(
        src_ref=edges.at[1], dst_ref=above,
        send_sem=down_sems.at[0], recv_sem=down_sems.at[1],
        device_id=(face, jnp.minimum(tile + 1, tiles - 1)), device_id_type=MESH,
    )
    east = pltpu.make_async_remote_copy(
        src_ref=east_block, dst_ref=from_east.at[tiles - 1 - tile],
        send_sem=east_send, recv_sem=east_recv.at[tile],
        device_id=(following, 0), device_id_type=MESH,
    )

    def seam_copy(other):
        return pltpu.make_async_remote_copy(
            src_ref=seam_out.at[other], dst_ref=seam_in,
            send_sem=seam_send.at[other], recv_sem=seam_recv,
            device_id=(preceding, other), device_id_type=MESH,
        )

    @pl.when(is_first)
    def _():
        def one(other, _):
            seam_copy(other).start()
            return 0

        lax.fori_loop(0, tiles, one, 0)

    east.start()

    @pl.when(jnp.logical_not(is_first))
    def _():
        up.start()

    @pl.when(jnp.logical_not(is_last))
    def _():
        down.start()

    @pl.when(jnp.logical_not(is_last))
    def _():
        up.wait_recv()
        south[...] = below[...]
        down.wait_send()

    @pl.when(is_last)
    def _():
        south[...] = jnp.zeros_like(south)

    @pl.when(jnp.logical_not(is_first))
    def _():
        down.wait_recv()
        north[...] = above[...]
        up.wait_send()

    east.wait_send()
    pltpu.make_async_remote_copy(
        src_ref=seam_out.at[0], dst_ref=seam_in,
        send_sem=seam_send.at[0], recv_sem=seam_recv,
        device_id=(following, 0), device_id_type=MESH,
    ).wait_recv()
    seam[...] = seam_in[...].astype(F32)

    @pl.when(is_first)
    def _():
        def one(other, _):
            seam_copy(other).wait_send()
            pltpu.make_async_remote_copy(
                src_ref=east_block, dst_ref=from_east.at[tiles - 1 - other],
                send_sem=east_send, recv_sem=east_recv.at[other],
                device_id=(preceding, other), device_id_type=MESH,
            ).wait_recv()
            return 0

        lax.fori_loop(0, tiles, one, 0)
        north[...] = from_east[...].reshape(side, width).astype(BF16)


def exchange_halo(normed, tiles, rows):
    cell_count, width = normed.shape
    side = cell_count // rows
    return pl.pallas_call(
        halo_kernel,
        out_shape=(
            jax.ShapeDtypeStruct((side, width), BF16),
            jax.ShapeDtypeStruct((side, width), BF16),
            jax.ShapeDtypeStruct((UNIT, width), F32),
        ),
        in_specs=[pl.BlockSpec(memory_space=pltpu.VMEM)],
        out_specs=[pl.BlockSpec(memory_space=pltpu.VMEM)] * 3,
        scratch_shapes=[
            pltpu.VMEM((2, side, width), BF16),
            pltpu.VMEM((rows, width), F32),
            pltpu.VMEM((tiles, UNIT, width), BF16),
            pltpu.VMEM((side, width), BF16),
            pltpu.VMEM((side, width), BF16),
            pltpu.VMEM((tiles, rows, width), F32),
            pltpu.VMEM((UNIT, width), BF16),
            pltpu.SemaphoreType.DMA((2,)),
            pltpu.SemaphoreType.DMA((2,)),
            pltpu.SemaphoreType.DMA,
            pltpu.SemaphoreType.DMA((tiles,)),
            pltpu.SemaphoreType.DMA((tiles,)),
            pltpu.SemaphoreType.DMA,
        ],
        compiler_params=pltpu.CompilerParams(
            collective_id=1, has_side_effects=True, vmem_limit_bytes=16 * MIB
        ),
        name="halo",
    )(normed)


def encode_kernel(
    normed, north, south, seam, grid, conv_weight, mlp_gain, mlp_in, mlp_out, out, planes
):
    side, width = north.shape
    cells = normed.shape[0]
    rows = cells // side
    per = 2
    hidden_step = 512

    def put(row, values):
        values = values.astype(F32)
        at = lax.broadcasted_iota(I32, (side, width), 0)
        left = jnp.where(at == 0, 0.0, pltpu.roll(values, 1, 0))
        right = jnp.where(at == side - 1, seam[pl.ds(row, 1), :], pltpu.roll(values, side - 1, 0))
        to = pl.ds(pl.multiple_of(row * side, side), side)
        planes[to, 0:width] = left.astype(BF16)
        planes[to, width : 2 * width] = values.astype(BF16)
        planes[to, 2 * width : 3 * width] = right.astype(BF16)

    put(0, north[...])
    put(rows + 1, south[...])

    def inner(row, _):
        put(row + 1, normed[pl.ds(pl.multiple_of(row * side, side), side), :])
        return 0

    lax.fori_loop(0, rows, inner, 0)

    def one(step, _):
        first = pl.multiple_of(step * (per * side), per * side)
        conv = None
        for tap in range(3):
            window = planes[pl.ds(pl.multiple_of(first + tap * side, side), per * side), :]
            term = dot(window, conv_weight[tap])
            conv = term if conv is None else conv + term
        mid = grid[pl.ds(first, per * side), :].astype(F32) + conv
        scale = lax.rsqrt(jnp.mean(mid * mid, axis=1, keepdims=True) + EPS)
        normed_two = (mid * scale * mlp_gain[...]).astype(BF16)
        result = mid
        for part in range(mlp_in.shape[1] // hidden_step):
            at = slice(part * hidden_step, (part + 1) * hidden_step)
            hidden = gelu(dot(normed_two, mlp_in[:, at])).astype(BF16)
            result = result + dot(hidden, mlp_out[at, :])
        out[pl.ds(first, per * side), :] = result.astype(BF16)
        return 0

    lax.fori_loop(0, rows // per, one, 0)


def encode(normed, north, south, seam, grid, conv_weight, mlp_gain, mlp_in, mlp_out):
    cell_count, width = normed.shape
    side = north.shape[0]
    vmem = pl.BlockSpec(memory_space=pltpu.VMEM)
    return pl.pallas_call(
        encode_kernel,
        out_shape=jax.ShapeDtypeStruct(normed.shape, BF16),
        in_specs=[vmem] * 9,
        out_specs=vmem,
        scratch_shapes=[pltpu.VMEM((cell_count + 2 * side, 3 * width), BF16)],
        compiler_params=pltpu.CompilerParams(vmem_limit_bytes=40 * MIB),
        name="encode",
    )(normed, north, south, seam, grid, conv_weight, mlp_gain, mlp_in, mlp_out)


def shards(
    state,
    obs_feat,
    obs_dest,
    obs_cell,
    obs_weight,
    obs_bias,
    obs_gain,
    norm_gain,
    conv_weight,
    mlp_gain,
    mlp_in,
    mlp_out,
):
    tiles = lax.axis_size("tile")
    devices = lax.axis_size("face") * tiles
    held = obs_feat.shape[0]
    capacity = 4 * held // devices
    rows, side, width = state.shape[2:]
    send, cells = pack(
        obs_dest.reshape(1, held), obs_cell.reshape(1, held), obs_feat, devices, capacity
    )
    faces = lax.axis_size("face")
    across = (faces, 4, tiles // 4)
    grid, normed = assimilate(
        send.reshape(send.shape[:1] + across + send.shape[2:]),
        cells.reshape(across + (1, 128)),
        state.reshape(rows * side, width),
        obs_weight,
        obs_bias.reshape(1, width),
        obs_gain.reshape(1, width),
        norm_gain.reshape(1, width),
    )
    north, south, seam = exchange_halo(normed, tiles, rows)
    result = encode(
        normed,
        north,
        south,
        seam,
        grid,
        conv_weight.reshape(3, 3 * width, width),
        mlp_gain.reshape(1, width),
        mlp_in,
        mlp_out,
    )
    return result.reshape(state.shape)


def solution(mesh):
    placed = (
        P("face", "tile", None, None, None),
        P(("face", "tile"), None),
        P(("face", "tile"), None),
        P(("face", "tile")),
    ) + (P(),) * 8
    return jax.shard_map(
        shards,
        mesh=mesh,
        in_specs=placed,
        out_specs=P("face", "tile", None, None, None),
        check_vma=False,
    )
```

```python
import math

import jax
import jax.numpy as jnp
from jax import lax
from jax.experimental import pallas as pl
from jax.experimental.pallas import tpu as pltpu
from jax.sharding import PartitionSpec as P

BF16 = jnp.bfloat16
F32 = jnp.float32
I32 = jnp.int32
MESH = pl.DeviceIdType.MESH
EPS = 1e-05
MIB = 2**20
UNIT = 16
BLOCK = 256


def gelu(x):
    inner = x * (math.sqrt(2.0 / math.pi) + (0.044715 * math.sqrt(2.0 / math.pi)) * (x * x))
    half = 0.5 * x
    return half + half * jnp.tanh(inner)


def gelu_narrow(x):
    x = x.astype(BF16)
    slope = BF16(math.sqrt(2.0 / math.pi))
    inner = x * (slope + BF16(0.044715 * math.sqrt(2.0 / math.pi)) * (x * x))
    half = BF16(0.5) * x
    return half + half * jnp.tanh(inner)


def ones_where(mask):
    return jnp.where(mask, 1.0, 0.0)


def dot(a, b):
    return jnp.dot(a, b, preferred_element_type=F32)


def dot_lanes(a, b):
    return lax.dot_general(a, b, (((1,), (1,)), ((), ())), preferred_element_type=F32)


def rank_kernel(dest, cell, rank, starts, cells):
    devices = starts.shape[1]
    rows = dest.shape[1]
    hot = lax.broadcasted_iota(I32, (devices, rows), 0) == dest[...]
    hot_f = ones_where(hot)
    hot_b = hot_f.astype(BF16)
    before = ones_where(
        lax.broadcasted_iota(I32, (BLOCK, BLOCK), 0) < lax.broadcasted_iota(I32, (BLOCK, BLOCK), 1)
    ).astype(BF16)
    ahead = jnp.zeros((devices, 1), F32)
    pieces = []
    for block in range(rows // BLOCK):
        at = slice(block * BLOCK, (block + 1) * BLOCK)
        pieces.append(dot(hot_b[:, at], before) + ahead)
        ahead = ahead + jnp.sum(hot_f[:, at], axis=1, keepdims=True)
    earlier = jnp.concatenate(pieces, axis=1)
    row_id = lax.broadcasted_iota(I32, (devices, devices), 0)
    col_id = lax.broadcasted_iota(I32, (devices, devices), 1)
    start = dot(
        ones_where(col_id < row_id).astype(BF16),
        jnp.broadcast_to(ahead, (devices, devices)).astype(BF16),
    )
    starts[...] = jnp.sum(jnp.where(row_id == col_id, start, 0.0), axis=0, keepdims=True).astype(I32)
    rank_in = jnp.sum(hot_f * earlier, axis=0, keepdims=True).astype(I32)
    rank[...] = jnp.sum(hot_f * (earlier + start[:, :1]), axis=0, keepdims=True).astype(I32)
    spot = cell[...] + 1
    high = hot_f * (spot // 128).astype(F32)
    low = hot_f * (spot % 128).astype(F32)
    in_slot = ones_where(lax.broadcasted_iota(I32, (128, rows), 0) == rank_in).astype(BF16)
    split = dot_lanes(jnp.concatenate([high, low], axis=0).astype(BF16), in_slot)
    cells[...] = (split[:devices] * 128.0 + split[devices:]).astype(I32)


def cut_kernel(starts, rank, feat, send, ordered):
    parts, devices = send.shape[:2]
    rows = feat.shape[0]
    capacity = parts * UNIT

    def sort_block(block, _):
        first = pl.multiple_of(block * BLOCK, BLOCK)
        chosen = ones_where(
            lax.broadcasted_iota(I32, (BLOCK, rows), 0) + first == rank[...]
        ).astype(BF16)
        ordered[pl.ds(first, BLOCK), :] = dot(chosen, feat[...])
        return 0

    lax.fori_loop(0, rows // BLOCK, sort_block, 0)
    ordered[rows:, :] = jnp.zeros((ordered.shape[0] - rows, feat.shape[1]), F32)

    def cut(target, _):
        values = ordered[pl.ds(starts[0, target], capacity), :]
        values = values.astype(BF16)
        for part in range(parts):
            send[part, target] = values[part * UNIT : (part + 1) * UNIT]
        return 0

    lax.fori_loop(0, devices, cut, 0, unroll=4)


def pack(dest, cell, feat, devices, capacity):
    rows, width = feat.shape
    vmem = pl.BlockSpec(memory_space=pltpu.VMEM)
    rank, starts, cells = pl.pallas_call(
        rank_kernel,
        out_shape=(
            jax.ShapeDtypeStruct((1, rows), I32),
            jax.ShapeDtypeStruct((1, devices), I32),
            jax.ShapeDtypeStruct((devices, 128), I32),
        ),
        in_specs=[vmem] * 2,
        out_specs=[vmem] * 3,
        compiler_params=pltpu.CompilerParams(vmem_limit_bytes=16 * MIB),
        name="rank",
    )(dest, cell)
    send = pl.pallas_call(
        cut_kernel,
        out_shape=jax.ShapeDtypeStruct((capacity // UNIT, devices, UNIT, width), BF16),
        in_specs=[pl.BlockSpec(memory_space=pltpu.SMEM), vmem, vmem],
        out_specs=vmem,
        scratch_shapes=[pltpu.VMEM((rows + 2 * capacity, width), F32)],
        compiler_params=pltpu.CompilerParams(vmem_limit_bytes=16 * MIB),
        name="cut",
    )(starts, rank, feat)
    return send, cells


def spread_cells(cells, part):
    sources = cells.shape[0]
    lane = lax.broadcasted_iota(I32, (128, 128), 1)
    pick = ones_where(
        lax.broadcasted_iota(I32, (128, 128), 0) == lane % UNIT + part * UNIT
    ).astype(BF16)
    high = dot((cells // 128).astype(F32).astype(BF16), pick)
    low = dot((cells % 128).astype(F32).astype(BF16), pick)
    value = high * 128.0 + low
    keep = lax.broadcasted_iota(I32, (sources, 128), 1) // UNIT == (
        lax.broadcasted_iota(I32, (sources, 128), 0) % 8
    )
    value = jnp.where(keep, value, 0.0).reshape(sources // 8, 8, 128)
    return jnp.sum(value, axis=1).astype(I32) - 1


def match_rows(ids, row):
    wide = jnp.broadcast_to(row, (UNIT, 128)).astype(BF16)
    wide = jnp.concatenate([wide] * (128 // UNIT), axis=0)
    return jnp.where(ids == wide, jnp.ones_like(ids), jnp.zeros_like(ids))


def embed_block(feats, block, weight, bias, embed):
    at = pl.ds(pl.multiple_of(block * 512, 512), 512)
    rows = feats[pl.ds(block * (512 // UNIT), 512 // UNIT)].reshape(512, feats.shape[-1])
    embed[at, :] = gelu_narrow(dot(rows, weight[...]) + bias[...])


def add_part(spots, embed, total, count, beside):
    groups = spots.shape[0]
    ids = lax.broadcasted_iota(I32, (128, 128), 0).astype(F32).astype(BF16)
    spot = spots[...]
    high = lax.shift_right_arithmetic(spot, 7)
    low = jnp.where(spot < 0, -1, spot - high * 128).astype(F32)

    def matches(rows):
        return jnp.concatenate(
            [match_rows(ids, rows[group : group + 1, :]) for group in range(groups)], axis=1
        )

    count[...] += dot_lanes(matches(low), matches(high.astype(F32)))
    per = 8

    def cell_block(block, _):
        beside(2 * block)
        beside(2 * block + 1)
        match = jnp.concatenate(
            [matches(jnp.where(high == block * per + part, low, -1.0)) for part in range(per)],
            axis=0,
        )
        at = pl.ds(pl.multiple_of(block * (per * 128), per * 128), per * 128)
        total[at, :] += dot(match, embed[...])
        return 0

    lax.fori_loop(0, total.shape[0] // (per * 128), cell_block, 0)


def finish_block(block, state, obs_gain, norm_gain, total, count, grid, normed):
    lane = lax.broadcasted_iota(I32, count.shape, 1)
    at = pl.ds(pl.multiple_of(block * 128, 128), 128)
    number = jnp.sum(jnp.where(lane == block, count[...], 0.0), axis=1, keepdims=True)
    number = jnp.maximum(number, 1.0)
    value = state[at, :].astype(F32) + obs_gain[...] * (total[at, :] * (1.0 / number))
    rounded = value.astype(BF16)
    grid[at, :] = rounded
    value = rounded.astype(F32)
    scale = lax.rsqrt(jnp.mean(value * value, axis=1, keepdims=True) + EPS)
    normed[at, :] = (value * scale * norm_gain[...]).astype(BF16)


class Halo:
    def __init__(
        self, barrier, normed, north, south, seam, edges, east_block, seam_out, above, below,
        from_east, seam_in, up_sems, down_sems, east_send, east_recv, seam_send, seam_recv,
    ):
        faces, tiles = lax.axis_size("face"), lax.axis_size("tile")
        face, tile = lax.axis_index("face"), lax.axis_index("tile")
        cell_count, width = normed.shape
        side = above.shape[0]
        rows = cell_count // side
        following, preceding = lax.rem(face + 1, faces), lax.rem(face + faces - 1, faces)
        is_first, is_last = tile == 0, tile == tiles - 1

        def remote(source, target, send_sem, recv_sem, device):
            return pltpu.make_async_remote_copy(
                src_ref=source, dst_ref=target, send_sem=send_sem, recv_sem=recv_sem,
                device_id=device, device_id_type=MESH,
            )

        up = remote(
            edges.at[0], below, up_sems.at[0], up_sems.at[1], (face, jnp.maximum(tile - 1, 0))
        )
        down = remote(
            edges.at[1], above, down_sems.at[0], down_sems.at[1],
            (face, jnp.minimum(tile + 1, tiles - 1)),
        )

        def east(other, device):
            return remote(
                east_block, from_east.at[tiles - 1 - other], east_send, east_recv.at[other], device
            )

        def seam_copy(other, device):
            return remote(
                seam_out.at[other], seam_in, seam_send.at[other], seam_recv, device
            )

        def each_tile(body):
            def one(other, _):
                body(other)
                return 0

            lax.fori_loop(0, tiles, one, 0)

        def greet_one(who):
            pl.semaphore_signal(barrier, inc=1, device_id=who, device_id_type=MESH)

        def greet():
            greet_one((following, 0))

            @pl.when(jnp.logical_not(is_first))
            def _():
                greet_one((face, tile - 1))

            @pl.when(jnp.logical_not(is_last))
            def _():
                greet_one((face, tile + 1))

            @pl.when(is_first)
            def _():
                each_tile(lambda other: greet_one((preceding, other)))

            return 1 + jnp.where(is_first, tiles, 1) + jnp.where(is_last, 0, 1)

        def start_first():
            edges[0] = normed[0:side, :]

            @pl.when(is_first)
            def _():
                slot = lax.broadcasted_iota(I32, (tiles * UNIT, side), 0)
                want = side - 1 - (slot // UNIT * rows - 1 + slot % UNIT)
                chosen = ones_where(lax.broadcasted_iota(I32, (tiles * UNIT, side), 1) == want)
                seam_out[...] = dot(chosen.astype(BF16), edges[0]).astype(BF16).reshape(
                    tiles, UNIT, width
                )
                each_tile(lambda other: seam_copy(other, (preceding, other)).start())

            @pl.when(jnp.logical_not(is_first))
            def _():
                up.start()

        def start_last():
            edges[1] = normed[cell_count - side : cell_count, :]

            @pl.when(jnp.logical_not(is_last))
            def _():
                down.start()

            for row in range(rows):
                last = normed[(rows - row) * side - 16 : (rows - row) * side, :].astype(F32)
                east_block[row : row + 1, :] = last[15:16, :]
            east(tile, (following, 0)).start()

        def finish():
            @pl.when(jnp.logical_not(is_last))
            def _():
                up.wait_recv()
                south[...] = below[...]
                down.wait_send()

            @pl.when(is_last)
            def _():
                south[...] = jnp.zeros_like(south)

            @pl.when(jnp.logical_not(is_first))
            def _():
                down.wait_recv()
                north[...] = above[...]
                up.wait_send()

            east(tile, (following, 0)).wait_send()
            seam_copy(0, (following, 0)).wait_recv()
            seam[...] = seam_in[...].astype(F32)

            @pl.when(is_first)
            def _():
                def one(other):
                    seam_copy(other, (preceding, other)).wait_send()
                    east(other, (preceding, other)).wait_recv()

                each_tile(one)
                north[...] = from_east[...].reshape(side, width).astype(BF16)

        self.greet, self.finish = greet, finish
        self.start_first, self.start_last = start_first, start_last


def gather_kernel(
    send, cells, state, weight, bias, obs_gain, norm_gain, grid, normed, north, south, seam,
    held, cell_held, cell_flat, spots, embed_even, embed_odd, total, count,
    send_sems, recv_sems, own_sems, *halo_scratch,
):
    embeds = (embed_even, embed_odd)
    parts = send.shape[0]
    face, tile = lax.axis_index("face"), lax.axis_index("tile")
    sizes = send.shape[1:4]
    mine = (face, tile // sizes[2], lax.rem(tile, sizes[2]))
    barrier = pltpu.get_barrier_semaphore()

    def other(dim, step):
        place = list(mine)
        place[dim] = lax.rem(mine[dim] + step, sizes[dim])
        return place[dim], (place[0], place[1] * sizes[2] + place[2])

    for dim in range(3):
        def greet(step, _, dim=dim):
            pl.semaphore_signal(
                barrier, inc=1, device_id=other(dim, step)[1], device_id_type=MESH
            )
            return 0

        lax.fori_loop(1, sizes[dim], greet, 0)

    halo = Halo(barrier, normed, north, south, seam, *halo_scratch)
    partners = halo.greet()

    def dim_of(part, stage):
        return (part + stage) % 3

    def views(part, stage):
        if part == parts:
            source = cells if stage == 0 else cell_held.at[stage - 1]
            return source, cell_held.at[stage]
        source = send.at[part] if stage == 0 else held.at[stage - 1, part]
        return source, held.at[stage, part]

    def along(ref, dim, place):
        return ref.at[(slice(None),) * dim + (place,)]

    def copies(part, stage, step):
        dim = dim_of(part, stage)
        source, target = views(part, stage)
        place, device = other(dim, step)
        return pltpu.make_async_remote_copy(
            src_ref=along(source, dim, place),
            dst_ref=along(target, dim, mine[dim]),
            send_sem=send_sems.at[part * 3 + stage, step],
            recv_sem=recv_sems.at[part * 3 + stage, step],
            device_id=device,
            device_id_type=MESH,
        )

    def own(part, stage):
        dim = dim_of(part, stage)
        source, target = views(part, stage)
        return pltpu.make_async_copy(
            along(source, dim, mine[dim]), along(target, dim, mine[dim]),
            own_sems.at[part * 3 + stage],
        )

    def start(part, stage):
        def one(step, _):
            copies(part, stage, step).start()
            return 0

        lax.fori_loop(1, sizes[dim_of(part, stage)], one, 0)
        own(part, stage).start()

    def finish(part, stage):
        def one(step, _):
            copies(part, stage, step).wait()
            return 0

        own(part, stage).wait()
        lax.fori_loop(1, sizes[dim_of(part, stage)], one, 0)

    def advance(which, stage):
        for part in which:
            finish(part, stage)
            start(part, stage + 1)

    def embed_part(part, block):
        feats = held.at[2, part]
        flat = feats.reshape(sizes[0] * sizes[1] * sizes[2], UNIT, send.shape[-1])
        embed_block(flat, block, weight, bias, embeds[part % 2])

    def add(part, _=None, more=True):
        def beside(block):
            if more:
                embed_part(part + 1, block)

        add_part(spots.at[part], embeds[part % 2], total, count, beside)
        return 0

    early, late = list(range(parts // 2)), list(range(parts // 2, parts))
    pl.semaphore_wait(barrier, sum(sizes) - 3 + partners)
    start(parts, 0)
    for part in early:
        start(part, 0)
    total[...] = jnp.zeros_like(total)
    count[...] = jnp.zeros_like(count)
    advance([parts], 0)
    advance(early, 0)
    advance([parts], 1)
    for part in late:
        start(part, 0)
    finish(parts, 2)

    def lay(row, _):
        across = sizes[1] * sizes[2]
        cell_flat[pl.ds(row, 1), :] = cell_held[
            2, row // across, lax.rem(row, across) // sizes[2], lax.rem(row, sizes[2])
        ]
        return 0

    lax.fori_loop(0, cell_flat.shape[0], lay, 0)
    advance(early, 1)
    for part in range(parts):
        spots[part] = spread_cells(cell_flat[...], part)
    for part in early:
        finish(part, 2)
    advance(late, 0)
    for block in range(4):
        embed_part(0, block)
    add(0)
    advance(late, 1)
    for part in early[1:-1]:
        add(part)
    for part in late:
        finish(part, 2)
    for part in [early[-1]] + late[:-1]:
        add(part)
    add(late[-1], more=False)

    def finish_grid(block):
        finish_block(block, state, obs_gain, norm_gain, total, count, grid, normed)

    def last_half(row, _):
        finish_grid(2 * row + 1)
        return 0

    def first_half(row, _):
        finish_grid(2 * row)
        return 0

    rows = total.shape[0] // 256
    last_half(0, 0)
    first_half(0, 0)
    halo.start_first()
    lax.fori_loop(1, rows, last_half, 0, unroll=rows - 1)
    first_half(rows - 1, 0)
    halo.start_last()
    lax.fori_loop(1, rows - 1, first_half, 0, unroll=rows - 2)
    halo.finish()


def assimilate(send, cells, state, weight, bias, obs_gain, norm_gain, tiles, rows):
    cell_count, width = state.shape
    side = cell_count // rows
    parts = send.shape[0]
    sources = cells.shape[0] * cells.shape[1] * cells.shape[2]
    vmem = pl.BlockSpec(memory_space=pltpu.VMEM)
    longest = max(send.shape[1:4])
    return pl.pallas_call(
        gather_kernel,
        out_shape=(jax.ShapeDtypeStruct(state.shape, BF16),) * 2
        + (jax.ShapeDtypeStruct((side, width), BF16),) * 2
        + (jax.ShapeDtypeStruct((UNIT, width), F32),),
        in_specs=[vmem] * 7,
        out_specs=[vmem] * 5,
        scratch_shapes=[
            pltpu.VMEM((3,) + send.shape, BF16),
            pltpu.VMEM((3,) + cells.shape, I32),
            pltpu.VMEM((sources, 128), I32),
            pltpu.VMEM((parts, sources // 8, 128), I32),
            pltpu.VMEM((sources * UNIT, width), BF16),
            pltpu.VMEM((sources * UNIT, width), BF16),
            pltpu.VMEM((cell_count, width), F32),
            pltpu.VMEM((128, 128), F32),
            pltpu.SemaphoreType.DMA((parts * 3 + 3, longest)),
            pltpu.SemaphoreType.DMA((parts * 3 + 3, longest)),
            pltpu.SemaphoreType.DMA((parts * 3 + 3,)),
            pltpu.VMEM((2, side, width), BF16),
            pltpu.VMEM((rows, width), F32),
            pltpu.VMEM((tiles, UNIT, width), BF16),
            pltpu.VMEM((side, width), BF16),
            pltpu.VMEM((side, width), BF16),
            pltpu.VMEM((tiles, rows, width), F32),
            pltpu.VMEM((UNIT, width), BF16),
            pltpu.SemaphoreType.DMA((2,)),
            pltpu.SemaphoreType.DMA((2,)),
            pltpu.SemaphoreType.DMA,
            pltpu.SemaphoreType.DMA((tiles,)),
            pltpu.SemaphoreType.DMA((tiles,)),
            pltpu.SemaphoreType.DMA,
        ],
        compiler_params=pltpu.CompilerParams(
            collective_id=0, has_side_effects=True, vmem_limit_bytes=38 * MIB
        ),
        name="gather",
    )(send, cells, state, weight, bias, obs_gain, norm_gain)


def encode_kernel(
    normed, north, south, seam, grid, conv_weight, mlp_gain, mlp_in, mlp_out, out, planes
):
    side, width = north.shape
    cells = normed.shape[0]
    rows = cells // side
    per = 4
    hidden_step = 512

    def put(row, values):
        values = values.astype(F32)
        at = lax.broadcasted_iota(I32, (side, width), 0)
        left = jnp.where(at == 0, 0.0, pltpu.roll(values, 1, 0))
        right = jnp.where(at == side - 1, seam[pl.ds(row, 1), :], pltpu.roll(values, side - 1, 0))
        to = pl.ds(pl.multiple_of(row * side, side), side)
        planes[to, 0:width] = left.astype(BF16)
        planes[to, width : 2 * width] = values.astype(BF16)
        planes[to, 2 * width : 3 * width] = right.astype(BF16)

    put(0, north[...])
    put(rows + 1, south[...])

    def inner(row, _):
        put(row + 1, normed[pl.ds(pl.multiple_of(row * side, side), side), :])
        return 0

    lax.fori_loop(0, rows, inner, 0)

    def one(step, _):
        first = pl.multiple_of(step * (per * side), per * side)
        conv = None
        for tap in range(3):
            window = planes[pl.ds(pl.multiple_of(first + tap * side, side), per * side), :]
            term = dot(window, conv_weight[tap])
            conv = term if conv is None else conv + term
        mid = grid[pl.ds(first, per * side), :].astype(F32) + conv
        scale = lax.rsqrt(jnp.mean(mid * mid, axis=1, keepdims=True) + EPS)
        normed_two = (mid * scale * mlp_gain[...]).astype(BF16)
        result = mid
        for part in range(mlp_in.shape[1] // hidden_step):
            at = slice(part * hidden_step, (part + 1) * hidden_step)
            hidden = gelu_narrow(dot(normed_two, mlp_in[:, at]))
            result = result + dot(hidden, mlp_out[at, :])
        out[pl.ds(first, per * side), :] = result.astype(BF16)
        return 0

    lax.fori_loop(0, rows // per, one, 0)


def encode(normed, north, south, seam, grid, conv_weight, mlp_gain, mlp_in, mlp_out):
    cell_count, width = normed.shape
    side = north.shape[0]
    vmem = pl.BlockSpec(memory_space=pltpu.VMEM)
    return pl.pallas_call(
        encode_kernel,
        out_shape=jax.ShapeDtypeStruct(normed.shape, BF16),
        in_specs=[vmem] * 9,
        out_specs=vmem,
        scratch_shapes=[pltpu.VMEM((cell_count + 2 * side, 3 * width), BF16)],
        compiler_params=pltpu.CompilerParams(vmem_limit_bytes=40 * MIB),
        name="encode",
    )(normed, north, south, seam, grid, conv_weight, mlp_gain, mlp_in, mlp_out)


def shards(
    state,
    obs_feat,
    obs_dest,
    obs_cell,
    obs_weight,
    obs_bias,
    obs_gain,
    norm_gain,
    conv_weight,
    mlp_gain,
    mlp_in,
    mlp_out,
):
    tiles = lax.axis_size("tile")
    devices = lax.axis_size("face") * tiles
    held = obs_feat.shape[0]
    capacity = 4 * held // devices
    rows, side, width = state.shape[2:]
    send, cells = pack(
        obs_dest.reshape(1, held), obs_cell.reshape(1, held), obs_feat, devices, capacity
    )
    faces = lax.axis_size("face")
    across = (faces, 4, tiles // 4)
    grid, normed, north, south, seam = assimilate(
        send.reshape(send.shape[:1] + across + send.shape[2:]),
        cells.reshape(across + (1, 128)),
        state.reshape(rows * side, width),
        obs_weight,
        obs_bias.reshape(1, width),
        obs_gain.reshape(1, width),
        norm_gain.reshape(1, width),
        tiles,
        rows,
    )
    result = encode(
        normed,
        north,
        south,
        seam,
        grid,
        conv_weight.reshape(3, 3 * width, width),
        mlp_gain.reshape(1, width),
        mlp_in,
        mlp_out,
    )
    return result.reshape(state.shape)


def solution(mesh):
    placed = (
        P("face", "tile", None, None, None),
        P(("face", "tile"), None),
        P(("face", "tile"), None),
        P(("face", "tile")),
    ) + (P(),) * 8
    return jax.shard_map(
        shards,
        mesh=mesh,
        in_specs=placed,
        out_specs=P("face", "tile", None, None, None),
        check_vma=False,
    )
```

```python
import math

import jax
import jax.numpy as jnp
from jax import lax
from jax.experimental import pallas as pl
from jax.experimental.pallas import tpu as pltpu
from jax.sharding import PartitionSpec as P

BF16 = jnp.bfloat16
F32 = jnp.float32
I32 = jnp.int32
MESH = pl.DeviceIdType.MESH
EPS = 1e-05
MIB = 2**20
UNIT = 16
BLOCK = 256


def gelu(x):
    inner = x * (math.sqrt(2.0 / math.pi) + (0.044715 * math.sqrt(2.0 / math.pi)) * (x * x))
    half = 0.5 * x
    return half + half * jnp.tanh(inner)


def gelu_narrow(x):
    x = x.astype(BF16)
    slope = BF16(math.sqrt(2.0 / math.pi))
    inner = x * (slope + BF16(0.044715 * math.sqrt(2.0 / math.pi)) * (x * x))
    half = BF16(0.5) * x
    return half + half * jnp.tanh(inner)


def ones_where(mask):
    return jnp.where(mask, 1.0, 0.0)


def dot(a, b):
    return jnp.dot(a, b, preferred_element_type=F32)


def dot_lanes(a, b):
    return lax.dot_general(a, b, (((1,), (1,)), ((), ())), preferred_element_type=F32)


def rank_kernel(dest, cell, rank, starts, cells):
    devices = starts.shape[1]
    rows = dest.shape[1]
    hot = lax.broadcasted_iota(I32, (devices, rows), 0) == dest[...]
    hot_f = ones_where(hot)
    hot_b = hot_f.astype(BF16)
    before = ones_where(
        lax.broadcasted_iota(I32, (BLOCK, BLOCK), 0) < lax.broadcasted_iota(I32, (BLOCK, BLOCK), 1)
    ).astype(BF16)
    ahead = jnp.zeros((devices, 1), F32)
    pieces = []
    for block in range(rows // BLOCK):
        at = slice(block * BLOCK, (block + 1) * BLOCK)
        pieces.append(dot(hot_b[:, at], before) + ahead)
        ahead = ahead + jnp.sum(hot_f[:, at], axis=1, keepdims=True)
    earlier = jnp.concatenate(pieces, axis=1)
    row_id = lax.broadcasted_iota(I32, (devices, devices), 0)
    col_id = lax.broadcasted_iota(I32, (devices, devices), 1)
    start = dot(
        ones_where(col_id < row_id).astype(BF16),
        jnp.broadcast_to(ahead, (devices, devices)).astype(BF16),
    )
    starts[...] = jnp.sum(jnp.where(row_id == col_id, start, 0.0), axis=0, keepdims=True).astype(I32)
    rank_in = jnp.sum(hot_f * earlier, axis=0, keepdims=True).astype(I32)
    rank[...] = jnp.sum(hot_f * (earlier + start[:, :1]), axis=0, keepdims=True).astype(I32)
    spot = cell[...] + 1
    high = hot_f * (spot // 128).astype(F32)
    low = hot_f * (spot % 128).astype(F32)
    in_slot = ones_where(lax.broadcasted_iota(I32, (128, rows), 0) == rank_in).astype(BF16)
    split = dot_lanes(jnp.concatenate([high, low], axis=0).astype(BF16), in_slot)
    cells[...] = (split[:devices] * 128.0 + split[devices:]).astype(I32)


def cut_kernel(starts, rank, feat, send, ordered):
    parts, devices = send.shape[:2]
    rows = feat.shape[0]
    capacity = parts * UNIT

    tall = 1024
    ids = lax.broadcasted_iota(I32, (128, 128), 0).astype(F32).astype(BF16)

    def sort_block(block, _):
        first = pl.multiple_of(block * tall, tall)
        chosen = []
        for part in range(tall // 128):
            place = rank[...] - (first + part * 128)
            place = jnp.where((place >= 0) & (place < 128), place, -1).astype(F32)
            chosen.append(
                jnp.concatenate(
                    [match_rows(ids, place[:, at : at + 128]) for at in range(0, rows, 128)], axis=1
                )
            )
        ordered[pl.ds(first, tall), :] = dot(jnp.concatenate(chosen, axis=0), feat[...])
        return 0

    lax.fori_loop(0, rows // tall, sort_block, 0)
    ordered[rows:, :] = jnp.zeros((ordered.shape[0] - rows, feat.shape[1]), F32)

    def cut(target, _):
        values = ordered[pl.ds(starts[0, target], capacity), :]
        values = values.astype(BF16)
        for part in range(parts):
            send[part, target] = values[part * UNIT : (part + 1) * UNIT]
        return 0

    lax.fori_loop(0, devices, cut, 0, unroll=4)


def pack(dest, cell, feat, devices, capacity):
    rows, width = feat.shape
    vmem = pl.BlockSpec(memory_space=pltpu.VMEM)
    rank, starts, cells = pl.pallas_call(
        rank_kernel,
        out_shape=(
            jax.ShapeDtypeStruct((1, rows), I32),
            jax.ShapeDtypeStruct((1, devices), I32),
            jax.ShapeDtypeStruct((devices, 128), I32),
        ),
        in_specs=[vmem] * 2,
        out_specs=[vmem] * 3,
        compiler_params=pltpu.CompilerParams(vmem_limit_bytes=16 * MIB),
        name="rank",
    )(dest, cell)
    send = pl.pallas_call(
        cut_kernel,
        out_shape=jax.ShapeDtypeStruct((capacity // UNIT, devices, UNIT, width), BF16),
        in_specs=[pl.BlockSpec(memory_space=pltpu.SMEM), vmem, vmem],
        out_specs=vmem,
        scratch_shapes=[pltpu.VMEM((rows + 2 * capacity, width), F32)],
        compiler_params=pltpu.CompilerParams(vmem_limit_bytes=24 * MIB),
        name="cut",
    )(starts, rank, feat)
    return send, cells


def spread_cells(cells, part):
    sources = cells.shape[0]
    lane = lax.broadcasted_iota(I32, (128, 128), 1)
    pick = ones_where(
        lax.broadcasted_iota(I32, (128, 128), 0) == lane % UNIT + part * UNIT
    ).astype(BF16)
    high = dot((cells // 128).astype(F32).astype(BF16), pick)
    low = dot((cells % 128).astype(F32).astype(BF16), pick)
    value = high * 128.0 + low
    keep = lax.broadcasted_iota(I32, (sources, 128), 1) // UNIT == (
        lax.broadcasted_iota(I32, (sources, 128), 0) % 8
    )
    value = jnp.where(keep, value, 0.0).reshape(sources // 8, 8, 128)
    return jnp.sum(value, axis=1).astype(I32) - 1


def match_rows(ids, row):
    wide = jnp.broadcast_to(row, (UNIT, 128)).astype(BF16)
    wide = jnp.concatenate([wide] * (128 // UNIT), axis=0)
    return jnp.where(ids == wide, jnp.ones_like(ids), jnp.zeros_like(ids))


def embed_block(feats, block, weight, bias, embed):
    at = pl.ds(pl.multiple_of(block * 512, 512), 512)
    rows = feats[pl.ds(block * (512 // UNIT), 512 // UNIT)].reshape(512, feats.shape[-1])
    embed[at, :] = gelu_narrow(dot(rows, weight[...]) + bias[...])


def add_part(spots, embed, total, count, beside):
    groups = spots.shape[0]
    ids = lax.broadcasted_iota(I32, (128, 128), 0).astype(F32).astype(BF16)
    spot = spots[...]
    high = lax.shift_right_arithmetic(spot, 7)
    low = jnp.where(spot < 0, -1, spot - high * 128).astype(F32)

    def matches(rows):
        return jnp.concatenate(
            [match_rows(ids, rows[group : group + 1, :]) for group in range(groups)], axis=1
        )

    count[...] += dot_lanes(matches(low), matches(high.astype(F32)))
    per = 8

    def cell_block(block, _):
        beside(2 * block)
        beside(2 * block + 1)
        match = jnp.concatenate(
            [matches(jnp.where(high == block * per + part, low, -1.0)) for part in range(per)],
            axis=0,
        )
        at = pl.ds(pl.multiple_of(block * (per * 128), per * 128), per * 128)
        total[at, :] += dot(match, embed[...])
        return 0

    lax.fori_loop(0, total.shape[0] // (per * 128), cell_block, 0)


def finish_block(block, state, obs_gain, norm_gain, total, count, grid, normed):
    lane = lax.broadcasted_iota(I32, count.shape, 1)
    at = pl.ds(pl.multiple_of(block * 128, 128), 128)
    number = jnp.sum(jnp.where(lane == block, count[...], 0.0), axis=1, keepdims=True)
    number = jnp.maximum(number, 1.0)
    value = state[at, :].astype(F32) + obs_gain[...] * (total[at, :] * (1.0 / number))
    rounded = value.astype(BF16)
    grid[at, :] = rounded
    value = rounded.astype(F32)
    scale = lax.rsqrt(jnp.mean(value * value, axis=1, keepdims=True) + EPS)
    normed[at, :] = (value * scale * norm_gain[...]).astype(BF16)


class Halo:
    def __init__(
        self, barrier, normed, north, south, seam, edges, east_block, seam_out, above, below,
        from_east, seam_in, up_sems, down_sems, east_send, east_recv, seam_send, seam_recv,
    ):
        faces, tiles = lax.axis_size("face"), lax.axis_size("tile")
        face, tile = lax.axis_index("face"), lax.axis_index("tile")
        cell_count, width = normed.shape
        side = above.shape[0]
        rows = cell_count // side
        following, preceding = lax.rem(face + 1, faces), lax.rem(face + faces - 1, faces)
        is_first, is_last = tile == 0, tile == tiles - 1

        def remote(source, target, send_sem, recv_sem, device):
            return pltpu.make_async_remote_copy(
                src_ref=source, dst_ref=target, send_sem=send_sem, recv_sem=recv_sem,
                device_id=device, device_id_type=MESH,
            )

        up = remote(
            edges.at[0], below, up_sems.at[0], up_sems.at[1], (face, jnp.maximum(tile - 1, 0))
        )
        down = remote(
            edges.at[1], above, down_sems.at[0], down_sems.at[1],
            (face, jnp.minimum(tile + 1, tiles - 1)),
        )

        def east(other, device):
            return remote(
                east_block, from_east.at[tiles - 1 - other], east_send, east_recv.at[other], device
            )

        def seam_copy(other, device):
            return remote(
                seam_out.at[other], seam_in, seam_send.at[other], seam_recv, device
            )

        def each_tile(body):
            def one(other, _):
                body(other)
                return 0

            lax.fori_loop(0, tiles, one, 0)

        def greet_one(who):
            pl.semaphore_signal(barrier, inc=1, device_id=who, device_id_type=MESH)

        def greet():
            greet_one((following, 0))

            @pl.when(jnp.logical_not(is_first))
            def _():
                greet_one((face, tile - 1))

            @pl.when(jnp.logical_not(is_last))
            def _():
                greet_one((face, tile + 1))

            @pl.when(is_first)
            def _():
                each_tile(lambda other: greet_one((preceding, other)))

            return 1 + jnp.where(is_first, tiles, 1) + jnp.where(is_last, 0, 1)

        def start_first():
            edges[0] = normed[0:side, :]

            @pl.when(is_first)
            def _():
                slot = lax.broadcasted_iota(I32, (tiles * UNIT, side), 0)
                want = side - 1 - (slot // UNIT * rows - 1 + slot % UNIT)
                chosen = ones_where(lax.broadcasted_iota(I32, (tiles * UNIT, side), 1) == want)
                seam_out[...] = dot(chosen.astype(BF16), edges[0]).astype(BF16).reshape(
                    tiles, UNIT, width
                )
                each_tile(lambda other: seam_copy(other, (preceding, other)).start())

            @pl.when(jnp.logical_not(is_first))
            def _():
                up.start()

        def start_last():
            edges[1] = normed[cell_count - side : cell_count, :]

            @pl.when(jnp.logical_not(is_last))
            def _():
                down.start()

            for row in range(rows):
                last = normed[(rows - row) * side - 16 : (rows - row) * side, :].astype(F32)
                east_block[row : row + 1, :] = last[15:16, :]
            east(tile, (following, 0)).start()

        def finish():
            @pl.when(jnp.logical_not(is_last))
            def _():
                up.wait_recv()
                south[...] = below[...]
                down.wait_send()

            @pl.when(is_last)
            def _():
                south[...] = jnp.zeros_like(south)

            @pl.when(jnp.logical_not(is_first))
            def _():
                down.wait_recv()
                north[...] = above[...]
                up.wait_send()

            east(tile, (following, 0)).wait_send()
            seam_copy(0, (following, 0)).wait_recv()
            seam[...] = seam_in[...].astype(F32)

            @pl.when(is_first)
            def _():
                def one(other):
                    seam_copy(other, (preceding, other)).wait_send()
                    east(other, (preceding, other)).wait_recv()

                each_tile(one)
                north[...] = from_east[...].reshape(side, width).astype(BF16)

        self.greet, self.finish = greet, finish
        self.start_first, self.start_last = start_first, start_last


def gather_kernel(
    send, cells, state, weight, bias, obs_gain, norm_gain, grid, normed, north, south, seam,
    held, cell_held, cell_flat, spots, embed_even, embed_odd, total, count,
    send_sems, recv_sems, own_sems, *halo_scratch,
):
    embeds = (embed_even, embed_odd)
    parts = send.shape[0]
    face, tile = lax.axis_index("face"), lax.axis_index("tile")
    sizes = send.shape[1:4]
    mine = (face, tile // sizes[2], lax.rem(tile, sizes[2]))
    barrier = pltpu.get_barrier_semaphore()

    def other(dim, step):
        place = list(mine)
        place[dim] = lax.rem(mine[dim] + step, sizes[dim])
        return place[dim], (place[0], place[1] * sizes[2] + place[2])

    for dim in range(3):
        def greet(step, _, dim=dim):
            pl.semaphore_signal(
                barrier, inc=1, device_id=other(dim, step)[1], device_id_type=MESH
            )
            return 0

        lax.fori_loop(1, sizes[dim], greet, 0)

    halo = Halo(barrier, normed, north, south, seam, *halo_scratch)
    partners = halo.greet()

    def dim_of(part, stage):
        return (part + stage) % 3

    def views(part, stage):
        if part == parts:
            source = cells if stage == 0 else cell_held.at[stage - 1]
            return source, cell_held.at[stage]
        source = send.at[part] if stage == 0 else held.at[stage - 1, part]
        return source, held.at[stage, part]

    def along(ref, dim, place):
        return ref.at[(slice(None),) * dim + (place,)]

    def copies(part, stage, step):
        dim = dim_of(part, stage)
        source, target = views(part, stage)
        place, device = other(dim, step)
        return pltpu.make_async_remote_copy(
            src_ref=along(source, dim, place),
            dst_ref=along(target, dim, mine[dim]),
            send_sem=send_sems.at[part * 3 + stage, step],
            recv_sem=recv_sems.at[part * 3 + stage, step],
            device_id=device,
            device_id_type=MESH,
        )

    def own(part, stage):
        dim = dim_of(part, stage)
        source, target = views(part, stage)
        return pltpu.make_async_copy(
            along(source, dim, mine[dim]), along(target, dim, mine[dim]),
            own_sems.at[part * 3 + stage],
        )

    def start(part, stage):
        def one(step, _):
            copies(part, stage, step).start()
            return 0

        lax.fori_loop(1, sizes[dim_of(part, stage)], one, 0)
        own(part, stage).start()

    def finish(part, stage):
        def one(step, _):
            copies(part, stage, step).wait()
            return 0

        own(part, stage).wait()
        lax.fori_loop(1, sizes[dim_of(part, stage)], one, 0)

    def advance(which, stage):
        for part in which:
            finish(part, stage)
            start(part, stage + 1)

    def embed_part(part, block):
        feats = held.at[2, part]
        flat = feats.reshape(sizes[0] * sizes[1] * sizes[2], UNIT, send.shape[-1])
        embed_block(flat, block, weight, bias, embeds[part % 2])

    def add(part, _=None, more=True):
        def beside(block):
            if more:
                embed_part(part + 1, block)

        add_part(spots.at[part], embeds[part % 2], total, count, beside)
        return 0

    early, late = list(range(parts // 2)), list(range(parts // 2, parts))
    pl.semaphore_wait(barrier, sum(sizes) - 3 + partners)
    start(parts, 0)
    for part in early:
        start(part, 0)
    total[...] = jnp.zeros_like(total)
    count[...] = jnp.zeros_like(count)
    advance([parts], 0)
    advance(early, 0)
    advance([parts], 1)
    for part in late:
        start(part, 0)
    finish(parts, 2)

    def lay(row, _):
        across = sizes[1] * sizes[2]
        cell_flat[pl.ds(row, 1), :] = cell_held[
            2, row // across, lax.rem(row, across) // sizes[2], lax.rem(row, sizes[2])
        ]
        return 0

    lax.fori_loop(0, cell_flat.shape[0], lay, 0)
    advance(early, 1)
    for part in range(parts):
        spots[part] = spread_cells(cell_flat[...], part)
    for part in early:
        finish(part, 2)
    advance(late, 0)
    for block in range(4):
        embed_part(0, block)
    add(0)
    advance(late, 1)
    for part in early[1:-1]:
        add(part)
    for part in late:
        finish(part, 2)
    for part in [early[-1]] + late[:-1]:
        add(part)
    add(late[-1], more=False)

    def finish_grid(block):
        finish_block(block, state, obs_gain, norm_gain, total, count, grid, normed)

    def last_half(row, _):
        finish_grid(2 * row + 1)
        return 0

    def first_half(row, _):
        finish_grid(2 * row)
        return 0

    rows = total.shape[0] // 256
    last_half(0, 0)
    first_half(0, 0)
    halo.start_first()
    lax.fori_loop(1, rows, last_half, 0, unroll=rows - 1)
    first_half(rows - 1, 0)
    halo.start_last()
    lax.fori_loop(1, rows - 1, first_half, 0, unroll=rows - 2)
    halo.finish()


def assimilate(send, cells, state, weight, bias, obs_gain, norm_gain, tiles, rows):
    cell_count, width = state.shape
    side = cell_count // rows
    parts = send.shape[0]
    sources = cells.shape[0] * cells.shape[1] * cells.shape[2]
    vmem = pl.BlockSpec(memory_space=pltpu.VMEM)
    longest = max(send.shape[1:4])
    return pl.pallas_call(
        gather_kernel,
        out_shape=(jax.ShapeDtypeStruct(state.shape, BF16),) * 2
        + (jax.ShapeDtypeStruct((side, width), BF16),) * 2
        + (jax.ShapeDtypeStruct((UNIT, width), F32),),
        in_specs=[vmem] * 7,
        out_specs=[vmem] * 5,
        scratch_shapes=[
            pltpu.VMEM((3,) + send.shape, BF16),
            pltpu.VMEM((3,) + cells.shape, I32),
            pltpu.VMEM((sources, 128), I32),
            pltpu.VMEM((parts, sources // 8, 128), I32),
            pltpu.VMEM((sources * UNIT, width), BF16),
            pltpu.VMEM((sources * UNIT, width), BF16),
            pltpu.VMEM((cell_count, width), F32),
            pltpu.VMEM((128, 128), F32),
            pltpu.SemaphoreType.DMA((parts * 3 + 3, longest)),
            pltpu.SemaphoreType.DMA((parts * 3 + 3, longest)),
            pltpu.SemaphoreType.DMA((parts * 3 + 3,)),
            pltpu.VMEM((2, side, width), BF16),
            pltpu.VMEM((rows, width), F32),
            pltpu.VMEM((tiles, UNIT, width), BF16),
            pltpu.VMEM((side, width), BF16),
            pltpu.VMEM((side, width), BF16),
            pltpu.VMEM((tiles, rows, width), F32),
            pltpu.VMEM((UNIT, width), BF16),
            pltpu.SemaphoreType.DMA((2,)),
            pltpu.SemaphoreType.DMA((2,)),
            pltpu.SemaphoreType.DMA,
            pltpu.SemaphoreType.DMA((tiles,)),
            pltpu.SemaphoreType.DMA((tiles,)),
            pltpu.SemaphoreType.DMA,
        ],
        compiler_params=pltpu.CompilerParams(
            collective_id=0, has_side_effects=True, vmem_limit_bytes=38 * MIB
        ),
        name="gather",
    )(send, cells, state, weight, bias, obs_gain, norm_gain)


def encode_kernel(
    normed, north, south, seam, grid, conv_weight, mlp_gain, mlp_in, mlp_out, out, planes
):
    side, width = north.shape
    cells = normed.shape[0]
    rows = cells // side
    per = 4
    hidden_step = 1024

    def put(row, values):
        values = values.astype(F32)
        at = lax.broadcasted_iota(I32, (side, width), 0)
        left = jnp.where(at == 0, 0.0, pltpu.roll(values, 1, 0))
        right = jnp.where(at == side - 1, seam[pl.ds(row, 1), :], pltpu.roll(values, side - 1, 0))
        to = pl.ds(pl.multiple_of(row * side, side), side)
        planes[to, 0:width] = left.astype(BF16)
        planes[to, width : 2 * width] = values.astype(BF16)
        planes[to, 2 * width : 3 * width] = right.astype(BF16)

    put(0, north[...])
    put(rows + 1, south[...])

    def inner(row, _):
        put(row + 1, normed[pl.ds(pl.multiple_of(row * side, side), side), :])
        return 0

    lax.fori_loop(0, rows, inner, 0)

    def one(step, _):
        first = pl.multiple_of(step * (per * side), per * side)
        conv = None
        for tap in range(3):
            window = planes[pl.ds(pl.multiple_of(first + tap * side, side), per * side), :]
            term = dot(window, conv_weight[tap])
            conv = term if conv is None else conv + term
        mid = grid[pl.ds(first, per * side), :].astype(F32) + conv
        scale = lax.rsqrt(jnp.mean(mid * mid, axis=1, keepdims=True) + EPS)
        normed_two = (mid * scale * mlp_gain[...]).astype(BF16)
        result = mid
        for part in range(mlp_in.shape[1] // hidden_step):
            at = slice(part * hidden_step, (part + 1) * hidden_step)
            hidden = gelu_narrow(dot(normed_two, mlp_in[:, at]))
            result = result + dot(hidden, mlp_out[at, :])
        out[pl.ds(first, per * side), :] = result.astype(BF16)
        return 0

    lax.fori_loop(0, rows // per, one, 0)


def encode(normed, north, south, seam, grid, conv_weight, mlp_gain, mlp_in, mlp_out):
    cell_count, width = normed.shape
    side = north.shape[0]
    vmem = pl.BlockSpec(memory_space=pltpu.VMEM)
    return pl.pallas_call(
        encode_kernel,
        out_shape=jax.ShapeDtypeStruct(normed.shape, BF16),
        in_specs=[vmem] * 9,
        out_specs=vmem,
        scratch_shapes=[pltpu.VMEM((cell_count + 2 * side, 3 * width), BF16)],
        compiler_params=pltpu.CompilerParams(vmem_limit_bytes=40 * MIB),
        name="encode",
    )(normed, north, south, seam, grid, conv_weight, mlp_gain, mlp_in, mlp_out)


def shards(
    state,
    obs_feat,
    obs_dest,
    obs_cell,
    obs_weight,
    obs_bias,
    obs_gain,
    norm_gain,
    conv_weight,
    mlp_gain,
    mlp_in,
    mlp_out,
):
    tiles = lax.axis_size("tile")
    devices = lax.axis_size("face") * tiles
    held = obs_feat.shape[0]
    capacity = 4 * held // devices
    rows, side, width = state.shape[2:]
    send, cells = pack(
        obs_dest.reshape(1, held), obs_cell.reshape(1, held), obs_feat, devices, capacity
    )
    faces = lax.axis_size("face")
    across = (faces, 4, tiles // 4)
    grid, normed, north, south, seam = assimilate(
        send.reshape(send.shape[:1] + across + send.shape[2:]),
        cells.reshape(across + (1, 128)),
        state.reshape(rows * side, width),
        obs_weight,
        obs_bias.reshape(1, width),
        obs_gain.reshape(1, width),
        norm_gain.reshape(1, width),
        tiles,
        rows,
    )
    result = encode(
        normed,
        north,
        south,
        seam,
        grid,
        conv_weight.reshape(3, 3 * width, width),
        mlp_gain.reshape(1, width),
        mlp_in,
        mlp_out,
    )
    return result.reshape(state.shape)


def solution(mesh):
    placed = (
        P("face", "tile", None, None, None),
        P(("face", "tile"), None),
        P(("face", "tile"), None),
        P(("face", "tile")),
    ) + (P(),) * 8
    return jax.shard_map(
        shards,
        mesh=mesh,
        in_specs=placed,
        out_specs=P("face", "tile", None, None, None),
        check_vma=False,
    )
```

```python
import math

import jax
import jax.numpy as jnp
from jax import lax
from jax.experimental import pallas as pl
from jax.experimental.pallas import tpu as pltpu
from jax.sharding import PartitionSpec as P

BF16 = jnp.bfloat16
F32 = jnp.float32
I32 = jnp.int32
MESH = pl.DeviceIdType.MESH
EPS = 1e-05
MIB = 2**20
UNIT = 16
BLOCK = 256


def gelu(x):
    inner = x * (math.sqrt(2.0 / math.pi) + (0.044715 * math.sqrt(2.0 / math.pi)) * (x * x))
    half = 0.5 * x
    return half + half * jnp.tanh(inner)


def gelu_narrow(x):
    x = x.astype(BF16)
    slope = BF16(math.sqrt(2.0 / math.pi))
    inner = x * (slope + BF16(0.044715 * math.sqrt(2.0 / math.pi)) * (x * x))
    half = BF16(0.5) * x
    return half + half * jnp.tanh(inner)


def ones_where(mask):
    return jnp.where(mask, 1.0, 0.0)


def dot(a, b):
    return jnp.dot(a, b, preferred_element_type=F32)


def dot_lanes(a, b):
    return lax.dot_general(a, b, (((1,), (1,)), ((), ())), preferred_element_type=F32)


def rank_kernel(dest, cell, rank, starts, cells):
    devices = starts.shape[1]
    rows = dest.shape[1]
    hot = lax.broadcasted_iota(I32, (devices, rows), 0) == dest[...]
    hot_f = ones_where(hot)
    hot_b = hot_f.astype(BF16)
    before = ones_where(
        lax.broadcasted_iota(I32, (BLOCK, BLOCK), 0) < lax.broadcasted_iota(I32, (BLOCK, BLOCK), 1)
    ).astype(BF16)
    ahead = jnp.zeros((devices, 1), F32)
    pieces = []
    for block in range(rows // BLOCK):
        at = slice(block * BLOCK, (block + 1) * BLOCK)
        pieces.append(dot(hot_b[:, at], before) + ahead)
        ahead = ahead + jnp.sum(hot_f[:, at], axis=1, keepdims=True)
    earlier = jnp.concatenate(pieces, axis=1)
    row_id = lax.broadcasted_iota(I32, (devices, devices), 0)
    col_id = lax.broadcasted_iota(I32, (devices, devices), 1)
    start = dot(
        ones_where(col_id < row_id).astype(BF16),
        jnp.broadcast_to(ahead, (devices, devices)).astype(BF16),
    )
    starts[...] = jnp.sum(jnp.where(row_id == col_id, start, 0.0), axis=0, keepdims=True).astype(I32)
    rank_in = jnp.sum(hot_f * earlier, axis=0, keepdims=True).astype(I32)
    rank[...] = jnp.sum(hot_f * (earlier + start[:, :1]), axis=0, keepdims=True).astype(I32)
    spot = cell[...] + 1
    high = hot_f * (spot // 128).astype(F32)
    low = hot_f * (spot % 128).astype(F32)
    in_slot = ones_where(lax.broadcasted_iota(I32, (128, rows), 0) == rank_in).astype(BF16)
    split = dot_lanes(jnp.concatenate([high, low], axis=0).astype(BF16), in_slot)
    cells[...] = (split[:devices] * 128.0 + split[devices:]).astype(I32)


def cut_kernel(starts, rank, feat, send, ordered):
    parts, devices = send.shape[:2]
    rows = feat.shape[0]
    capacity = parts * UNIT

    tall = 1024
    ids = lax.broadcasted_iota(I32, (128, 128), 0).astype(F32).astype(BF16)

    def sort_block(block, _):
        first = pl.multiple_of(block * tall, tall)
        chosen = []
        for part in range(tall // 128):
            place = rank[...] - (first + part * 128)
            place = jnp.where((place >= 0) & (place < 128), place, -1).astype(F32)
            chosen.append(
                jnp.concatenate(
                    [match_rows(ids, place[:, at : at + 128]) for at in range(0, rows, 128)], axis=1
                )
            )
        ordered[pl.ds(first, tall), :] = dot(jnp.concatenate(chosen, axis=0), feat[...])
        return 0

    lax.fori_loop(0, rows // tall, sort_block, 0)
    ordered[rows:, :] = jnp.zeros((ordered.shape[0] - rows, feat.shape[1]), F32)

    def cut(target, _):
        values = ordered[pl.ds(starts[0, target], capacity), :]
        values = values.astype(BF16)
        for part in range(parts):
            send[part, target] = values[part * UNIT : (part + 1) * UNIT]
        return 0

    lax.fori_loop(0, devices, cut, 0, unroll=4)


def pack(dest, cell, feat, devices, capacity):
    rows, width = feat.shape
    vmem = pl.BlockSpec(memory_space=pltpu.VMEM)
    rank, starts, cells = pl.pallas_call(
        rank_kernel,
        out_shape=(
            jax.ShapeDtypeStruct((1, rows), I32),
            jax.ShapeDtypeStruct((1, devices), I32),
            jax.ShapeDtypeStruct((devices, 128), I32),
        ),
        in_specs=[vmem] * 2,
        out_specs=[vmem] * 3,
        compiler_params=pltpu.CompilerParams(vmem_limit_bytes=16 * MIB),
        name="rank",
    )(dest, cell)
    send = pl.pallas_call(
        cut_kernel,
        out_shape=jax.ShapeDtypeStruct((capacity // UNIT, devices, UNIT, width), BF16),
        in_specs=[pl.BlockSpec(memory_space=pltpu.SMEM), vmem, vmem],
        out_specs=vmem,
        scratch_shapes=[pltpu.VMEM((rows + 2 * capacity, width), F32)],
        compiler_params=pltpu.CompilerParams(vmem_limit_bytes=24 * MIB),
        name="cut",
    )(starts, rank, feat)
    return send, cells


def spread_cells(cells, part):
    sources = cells.shape[0]
    lane = lax.broadcasted_iota(I32, (128, 128), 1)
    pick = ones_where(
        lax.broadcasted_iota(I32, (128, 128), 0) == lane % UNIT + part * UNIT
    ).astype(BF16)
    high = dot((cells // 128).astype(F32).astype(BF16), pick)
    low = dot((cells % 128).astype(F32).astype(BF16), pick)
    value = high * 128.0 + low
    keep = lax.broadcasted_iota(I32, (sources, 128), 1) // UNIT == (
        lax.broadcasted_iota(I32, (sources, 128), 0) % 8
    )
    value = jnp.where(keep, value, 0.0).reshape(sources // 8, 8, 128)
    return jnp.sum(value, axis=1).astype(I32) - 1


def match_rows(ids, row):
    wide = jnp.broadcast_to(row, (UNIT, 128)).astype(BF16)
    wide = jnp.concatenate([wide] * (128 // UNIT), axis=0)
    return jnp.where(ids == wide, jnp.ones_like(ids), jnp.zeros_like(ids))


def embed_block(feats, block, weight, bias, embed):
    at = pl.ds(pl.multiple_of(block * 512, 512), 512)
    rows = feats[pl.ds(block * (512 // UNIT), 512 // UNIT)].reshape(512, feats.shape[-1])
    embed[at, :] = gelu_narrow(dot(rows, weight[...]) + bias[...])


def add_part(spots, embed, total, count, beside):
    groups = spots.shape[0]
    ids = lax.broadcasted_iota(I32, (128, 128), 0).astype(F32).astype(BF16)
    spot = spots[...]
    high = lax.shift_right_arithmetic(spot, 7)
    low = jnp.where(spot < 0, -1, spot - high * 128).astype(F32)

    def matches(rows):
        return jnp.concatenate(
            [match_rows(ids, rows[group : group + 1, :]) for group in range(groups)], axis=1
        )

    count[...] += dot_lanes(matches(low), matches(high.astype(F32)))
    per = 8

    def cell_block(block, _):
        beside(2 * block)
        beside(2 * block + 1)
        match = jnp.concatenate(
            [matches(jnp.where(high == block * per + part, low, -1.0)) for part in range(per)],
            axis=0,
        )
        at = pl.ds(pl.multiple_of(block * (per * 128), per * 128), per * 128)
        total[at, :] += dot(match, embed[...])
        return 0

    lax.fori_loop(0, total.shape[0] // (per * 128), cell_block, 0)


def finish_block(block, state, obs_gain, norm_gain, total, count, grid, normed):
    lane = lax.broadcasted_iota(I32, count.shape, 1)
    at = pl.ds(pl.multiple_of(block * 128, 128), 128)
    number = jnp.sum(jnp.where(lane == block, count[...], 0.0), axis=1, keepdims=True)
    number = jnp.maximum(number, 1.0)
    value = state[at, :].astype(F32) + obs_gain[...] * (total[at, :] * (1.0 / number))
    rounded = value.astype(BF16)
    grid[at, :] = rounded
    value = rounded.astype(F32)
    scale = lax.rsqrt(jnp.mean(value * value, axis=1, keepdims=True) + EPS)
    normed[at, :] = (value * scale * norm_gain[...]).astype(BF16)


class Halo:
    def __init__(
        self, barrier, normed, north, south, seam, edges, east_block, seam_out, above, below,
        from_east, seam_in, up_sems, down_sems, east_send, east_recv, seam_send, seam_recv,
    ):
        faces, tiles = lax.axis_size("face"), lax.axis_size("tile")
        face, tile = lax.axis_index("face"), lax.axis_index("tile")
        cell_count, width = normed.shape
        side = above.shape[0]
        rows = cell_count // side
        following, preceding = lax.rem(face + 1, faces), lax.rem(face + faces - 1, faces)
        is_first, is_last = tile == 0, tile == tiles - 1

        def remote(source, target, send_sem, recv_sem, device):
            return pltpu.make_async_remote_copy(
                src_ref=source, dst_ref=target, send_sem=send_sem, recv_sem=recv_sem,
                device_id=device, device_id_type=MESH,
            )

        up = remote(
            edges.at[0], below, up_sems.at[0], up_sems.at[1], (face, jnp.maximum(tile - 1, 0))
        )
        down = remote(
            edges.at[1], above, down_sems.at[0], down_sems.at[1],
            (face, jnp.minimum(tile + 1, tiles - 1)),
        )

        def east(other, device):
            return remote(
                east_block, from_east.at[tiles - 1 - other], east_send, east_recv.at[other], device
            )

        def seam_copy(other, device):
            return remote(
                seam_out.at[other], seam_in, seam_send.at[other], seam_recv, device
            )

        def each_tile(body):
            def one(other, _):
                body(other)
                return 0

            lax.fori_loop(0, tiles, one, 0)

        def greet_one(who):
            pl.semaphore_signal(barrier, inc=1, device_id=who, device_id_type=MESH)

        def greet():
            greet_one((following, 0))

            @pl.when(jnp.logical_not(is_first))
            def _():
                greet_one((face, tile - 1))

            @pl.when(jnp.logical_not(is_last))
            def _():
                greet_one((face, tile + 1))

            @pl.when(is_first)
            def _():
                each_tile(lambda other: greet_one((preceding, other)))

            return 1 + jnp.where(is_first, tiles, 1) + jnp.where(is_last, 0, 1)

        def start_first():
            edges[0] = normed[0:side, :]

            @pl.when(is_first)
            def _():
                slot = lax.broadcasted_iota(I32, (tiles * UNIT, side), 0)
                want = side - 1 - (slot // UNIT * rows - 1 + slot % UNIT)
                chosen = ones_where(lax.broadcasted_iota(I32, (tiles * UNIT, side), 1) == want)
                seam_out[...] = dot(chosen.astype(BF16), edges[0]).astype(BF16).reshape(
                    tiles, UNIT, width
                )
                each_tile(lambda other: seam_copy(other, (preceding, other)).start())

            @pl.when(jnp.logical_not(is_first))
            def _():
                up.start()

        def start_last():
            edges[1] = normed[cell_count - side : cell_count, :]

            @pl.when(jnp.logical_not(is_last))
            def _():
                down.start()

            for row in range(rows):
                last = normed[(rows - row) * side - 16 : (rows - row) * side, :].astype(F32)
                east_block[row : row + 1, :] = last[15:16, :]
            east(tile, (following, 0)).start()

        def finish():
            @pl.when(jnp.logical_not(is_last))
            def _():
                up.wait_recv()
                south[...] = below[...]
                down.wait_send()

            @pl.when(is_last)
            def _():
                south[...] = jnp.zeros_like(south)

            @pl.when(jnp.logical_not(is_first))
            def _():
                down.wait_recv()
                north[...] = above[...]
                up.wait_send()

            east(tile, (following, 0)).wait_send()
            seam_copy(0, (following, 0)).wait_recv()
            seam[...] = seam_in[...].astype(F32)

            @pl.when(is_first)
            def _():
                def one(other):
                    seam_copy(other, (preceding, other)).wait_send()
                    east(other, (preceding, other)).wait_recv()

                each_tile(one)
                north[...] = from_east[...].reshape(side, width).astype(BF16)

        self.greet, self.finish = greet, finish
        self.start_first, self.start_last = start_first, start_last


def gather_kernel(
    send, cells, state, weight, bias, obs_gain, norm_gain, grid, normed, north, south, seam,
    held, cell_held, cell_flat, spots, embed_even, embed_odd, total, count,
    send_sems, recv_sems, own_sems, *halo_scratch,
):
    embeds = (embed_even, embed_odd)
    parts = send.shape[0]
    face, tile = lax.axis_index("face"), lax.axis_index("tile")
    sizes = send.shape[1:4]
    mine = (face, tile // sizes[2], lax.rem(tile, sizes[2]))
    barrier = pltpu.get_barrier_semaphore()

    def other(dim, step):
        place = list(mine)
        place[dim] = lax.rem(mine[dim] + step, sizes[dim])
        return place[dim], (place[0], place[1] * sizes[2] + place[2])

    for dim in range(3):
        def greet(step, _, dim=dim):
            pl.semaphore_signal(
                barrier, inc=1, device_id=other(dim, step)[1], device_id_type=MESH
            )
            return 0

        lax.fori_loop(1, sizes[dim], greet, 0)

    halo = Halo(barrier, normed, north, south, seam, *halo_scratch)
    partners = halo.greet()

    def dim_of(part, stage):
        return (part + stage) % 3

    def views(part, stage):
        if part == parts:
            source = cells if stage == 0 else cell_held.at[stage - 1]
            return source, cell_held.at[stage]
        source = send.at[part] if stage == 0 else held.at[stage - 1, part]
        return source, held.at[stage, part]

    def along(ref, dim, place):
        return ref.at[(slice(None),) * dim + (place,)]

    def copies(part, stage, step):
        dim = dim_of(part, stage)
        source, target = views(part, stage)
        place, device = other(dim, step)
        return pltpu.make_async_remote_copy(
            src_ref=along(source, dim, place),
            dst_ref=along(target, dim, mine[dim]),
            send_sem=send_sems.at[part * 3 + stage, step],
            recv_sem=recv_sems.at[part * 3 + stage, step],
            device_id=device,
            device_id_type=MESH,
        )

    def own(part, stage):
        dim = dim_of(part, stage)
        source, target = views(part, stage)
        return pltpu.make_async_copy(
            along(source, dim, mine[dim]), along(target, dim, mine[dim]),
            own_sems.at[part * 3 + stage],
        )

    def start(part, stage):
        def one(step, _):
            copies(part, stage, step).start()
            return 0

        lax.fori_loop(1, sizes[dim_of(part, stage)], one, 0)
        own(part, stage).start()

    def finish(part, stage):
        def one(step, _):
            copies(part, stage, step).wait()
            return 0

        own(part, stage).wait()
        lax.fori_loop(1, sizes[dim_of(part, stage)], one, 0)

    def advance(which, stage):
        for part in which:
            finish(part, stage)
            start(part, stage + 1)

    def embed_part(part, block):
        feats = held.at[2, part]
        flat = feats.reshape(sizes[0] * sizes[1] * sizes[2], UNIT, send.shape[-1])
        embed_block(flat, block, weight, bias, embeds[part % 2])

    def add(part, _=None, more=True):
        def beside(block):
            if more:
                embed_part(part + 1, block)

        add_part(spots.at[part], embeds[part % 2], total, count, beside)
        return 0

    early, late = list(range(parts // 2)), list(range(parts // 2, parts))
    pl.semaphore_wait(barrier, sum(sizes) - 3 + partners)
    start(parts, 0)
    for part in early:
        start(part, 0)
    total[...] = jnp.zeros_like(total)
    count[...] = jnp.zeros_like(count)
    advance([parts], 0)
    advance(early, 0)
    advance([parts], 1)
    for part in late:
        start(part, 0)
    advance(early, 1)
    finish(parts, 2)

    def lay(row, _):
        across = sizes[1] * sizes[2]
        cell_flat[pl.ds(row, 1), :] = cell_held[
            2, row // across, lax.rem(row, across) // sizes[2], lax.rem(row, sizes[2])
        ]
        return 0

    lax.fori_loop(0, cell_flat.shape[0], lay, 0, unroll=4)
    for part in range(parts):
        spots[part] = spread_cells(cell_flat[...], part)
    for part in early:
        finish(part, 2)
    advance(late, 0)
    for block in range(4):
        embed_part(0, block)
    add(0)
    advance(late, 1)
    for part in early[1:-1]:
        add(part)
    for part in late:
        finish(part, 2)
    for part in [early[-1]] + late[:-1]:
        add(part)
    add(late[-1], more=False)

    def finish_grid(block):
        finish_block(block, state, obs_gain, norm_gain, total, count, grid, normed)

    def last_half(row, _):
        finish_grid(2 * row + 1)
        return 0

    def first_half(row, _):
        finish_grid(2 * row)
        return 0

    rows = total.shape[0] // 256
    last_half(0, 0)
    first_half(0, 0)
    halo.start_first()
    lax.fori_loop(1, rows, last_half, 0, unroll=rows - 1)
    first_half(rows - 1, 0)
    halo.start_last()
    lax.fori_loop(1, rows - 1, first_half, 0, unroll=rows - 2)
    halo.finish()


def assimilate(send, cells, state, weight, bias, obs_gain, norm_gain, tiles, rows):
    cell_count, width = state.shape
    side = cell_count // rows
    parts = send.shape[0]
    sources = cells.shape[0] * cells.shape[1] * cells.shape[2]
    vmem = pl.BlockSpec(memory_space=pltpu.VMEM)
    longest = max(send.shape[1:4])
    return pl.pallas_call(
        gather_kernel,
        out_shape=(jax.ShapeDtypeStruct(state.shape, BF16),) * 2
        + (jax.ShapeDtypeStruct((side, width), BF16),) * 2
        + (jax.ShapeDtypeStruct((UNIT, width), F32),),
        in_specs=[vmem] * 7,
        out_specs=[vmem] * 5,
        scratch_shapes=[
            pltpu.VMEM((3,) + send.shape, BF16),
            pltpu.VMEM((3,) + cells.shape, I32),
            pltpu.VMEM((sources, 128), I32),
            pltpu.VMEM((parts, sources // 8, 128), I32),
            pltpu.VMEM((sources * UNIT, width), BF16),
            pltpu.VMEM((sources * UNIT, width), BF16),
            pltpu.VMEM((cell_count, width), F32),
            pltpu.VMEM((128, 128), F32),
            pltpu.SemaphoreType.DMA((parts * 3 + 3, longest)),
            pltpu.SemaphoreType.DMA((parts * 3 + 3, longest)),
            pltpu.SemaphoreType.DMA((parts * 3 + 3,)),
            pltpu.VMEM((2, side, width), BF16),
            pltpu.VMEM((rows, width), F32),
            pltpu.VMEM((tiles, UNIT, width), BF16),
            pltpu.VMEM((side, width), BF16),
            pltpu.VMEM((side, width), BF16),
            pltpu.VMEM((tiles, rows, width), F32),
            pltpu.VMEM((UNIT, width), BF16),
            pltpu.SemaphoreType.DMA((2,)),
            pltpu.SemaphoreType.DMA((2,)),
            pltpu.SemaphoreType.DMA,
            pltpu.SemaphoreType.DMA((tiles,)),
            pltpu.SemaphoreType.DMA((tiles,)),
            pltpu.SemaphoreType.DMA,
        ],
        compiler_params=pltpu.CompilerParams(
            collective_id=0, has_side_effects=True, vmem_limit_bytes=38 * MIB
        ),
        name="gather",
    )(send, cells, state, weight, bias, obs_gain, norm_gain)


def encode_kernel(
    normed, north, south, seam, grid, conv_weight, mlp_gain, mlp_in, mlp_out, out, planes
):
    side, width = north.shape
    cells = normed.shape[0]
    rows = cells // side
    per = 4
    hidden_step = 1024

    def put(row, values):
        values = values.astype(F32)
        at = lax.broadcasted_iota(I32, (side, width), 0)
        left = jnp.where(at == 0, 0.0, pltpu.roll(values, 1, 0))
        right = jnp.where(at == side - 1, seam[pl.ds(row, 1), :], pltpu.roll(values, side - 1, 0))
        to = pl.ds(pl.multiple_of(row * side, side), side)
        planes[to, 0:width] = left.astype(BF16)
        planes[to, width : 2 * width] = values.astype(BF16)
        planes[to, 2 * width : 3 * width] = right.astype(BF16)

    put(0, north[...])
    put(rows + 1, south[...])

    def inner(row, _):
        put(row + 1, normed[pl.ds(pl.multiple_of(row * side, side), side), :])
        return 0

    lax.fori_loop(0, rows, inner, 0)

    def one(step, _):
        first = pl.multiple_of(step * (per * side), per * side)
        conv = None
        for tap in range(3):
            window = planes[pl.ds(pl.multiple_of(first + tap * side, side), per * side), :]
            term = dot(window, conv_weight[tap])
            conv = term if conv is None else conv + term
        mid = grid[pl.ds(first, per * side), :].astype(F32) + conv
        scale = lax.rsqrt(jnp.mean(mid * mid, axis=1, keepdims=True) + EPS)
        normed_two = (mid * scale * mlp_gain[...]).astype(BF16)
        result = mid
        for part in range(mlp_in.shape[1] // hidden_step):
            at = slice(part * hidden_step, (part + 1) * hidden_step)
            hidden = gelu_narrow(dot(normed_two, mlp_in[:, at]))
            result = result + dot(hidden, mlp_out[at, :])
        out[pl.ds(first, per * side), :] = result.astype(BF16)
        return 0

    lax.fori_loop(0, rows // per, one, 0)


def encode(normed, north, south, seam, grid, conv_weight, mlp_gain, mlp_in, mlp_out):
    cell_count, width = normed.shape
    side = north.shape[0]
    vmem = pl.BlockSpec(memory_space=pltpu.VMEM)
    return pl.pallas_call(
        encode_kernel,
        out_shape=jax.ShapeDtypeStruct(normed.shape, BF16),
        in_specs=[vmem] * 9,
        out_specs=vmem,
        scratch_shapes=[pltpu.VMEM((cell_count + 2 * side, 3 * width), BF16)],
        compiler_params=pltpu.CompilerParams(vmem_limit_bytes=40 * MIB),
        name="encode",
    )(normed, north, south, seam, grid, conv_weight, mlp_gain, mlp_in, mlp_out)


def shards(
    state,
    obs_feat,
    obs_dest,
    obs_cell,
    obs_weight,
    obs_bias,
    obs_gain,
    norm_gain,
    conv_weight,
    mlp_gain,
    mlp_in,
    mlp_out,
):
    tiles = lax.axis_size("tile")
    devices = lax.axis_size("face") * tiles
    held = obs_feat.shape[0]
    capacity = 4 * held // devices
    rows, side, width = state.shape[2:]
    send, cells = pack(
        obs_dest.reshape(1, held), obs_cell.reshape(1, held), obs_feat, devices, capacity
    )
    faces = lax.axis_size("face")
    across = (faces, 4, tiles // 4)
    grid, normed, north, south, seam = assimilate(
        send.reshape(send.shape[:1] + across + send.shape[2:]),
        cells.reshape(across + (1, 128)),
        state.reshape(rows * side, width),
        obs_weight,
        obs_bias.reshape(1, width),
        obs_gain.reshape(1, width),
        norm_gain.reshape(1, width),
        tiles,
        rows,
    )
    result = encode(
        normed,
        north,
        south,
        seam,
        grid,
        conv_weight.reshape(3, 3 * width, width),
        mlp_gain.reshape(1, width),
        mlp_in,
        mlp_out,
    )
    return result.reshape(state.shape)


def solution(mesh):
    placed = (
        P("face", "tile", None, None, None),
        P(("face", "tile"), None),
        P(("face", "tile"), None),
        P(("face", "tile")),
    ) + (P(),) * 8
    return jax.shard_map(
        shards,
        mesh=mesh,
        in_specs=placed,
        out_specs=P("face", "tile", None, None, None),
        check_vma=False,
    )
```
